32 devices in a mesh: gx: 4 (over y, core), gy: 4 (over z), ga: 2 (over x).
Axes of the slice: x: 2, y: 2, z: 4, core: 2. Of those that a mesh axis runs over, the one named last changes fastest.
Arguments:
- offsets: float32 [3, 8, 8, 32, 128], P(None, 'gx', 'gy', 'ga'), may hold values from 0 to 1
- charge: float32 [8, 8, 32, 128], P('gx', 'gy', 'ga'), may hold values from -3 to 3
- counts: int32 [8, 8, 32], P('gx', 'gy', 'ga'), may hold values from 8 to 128, as said below
- partners: int32 [8, 8, 32, 128], P('gx', 'gy', 'ga'), may hold values from 0 to 127
Outputs:
- short_force: float32 [3, 8, 8, 32, 128], P(None, 'gx', 'gy', 'ga')
- long_force: float32 [3, 8, 8, 32, 128], P(None, 'gx', 'gy', 'ga')
The draws below stay inside these ranges and needn't reach their ends.
Inputs may be any that keep to these rules, and one draw needn't show every extreme that they name: `counts`: each cell holds at least 8 beads and at most 128; some cell holds exactly 128.
All inputs are finite; a program needn't handle non-finite values.
Results may differ from the reference program's by a relative error of at most 0.0003.
Values sent between devices are 32-bit elements; how exact they have to be, the bound alone decides.
A program may use at most 192 MiB of HBM per device.

```python
import jax
import jax.numpy as jnp
from jax import lax

TILE = 128
CELLS_X = 8
CELLS_Y = 8
CELLS_Z = 32


def draw_counts(key, part):
    drawn = jax.random.randint(key, (CELLS_X, CELLS_Y, CELLS_Z), 8, TILE + 1)
    return drawn.at[0, 0, 0].set(TILE).astype(jnp.int32)


def set_ends(result, rng, least, top_value):
    longest = result.shape.index(max(result.shape))
    spots = []
    for shift in (0, 1):
        where = [jax.random.randint(jax.random.fold_in(rng, axis), (), 0, length) for axis, length in enumerate(result.shape)]
        where[longest] = (where[longest] + shift) % result.shape[longest]
        spots.append(tuple(where))
    return result.at[spots[0]].set(least).at[spots[1]].set(top_value)


def block_scale(rng, shape, split, least, top_value):
    factor_of, own = 1.0, jax.random.fold_in(rng, 6)
    for axis_at, blocks in split:
        heights = jnp.exp(jax.random.uniform(jax.random.fold_in(own, axis_at), (blocks,), jnp.float32, least / len(split), top_value / len(split)))
        factor_of = factor_of * jnp.repeat(heights, shape[axis_at] // blocks).reshape([-1 if axis == axis_at else 1 for axis in range(len(shape))])
    return factor_of


def bell_draw(key, shape, scale, reach, pieces=(), held_as=jnp.bfloat16):
    factor_of = block_scale(key, shape, pieces, -0.22, 0.18) if pieces else 1.0
    values = jax.random.normal(key, shape, jnp.float32) * scale * factor_of
    return jnp.minimum(jnp.maximum(values, -reach), reach).astype(held_as)


def setup_inputs(seed: int = 0) -> dict:
    keys = jax.random.split(jax.random.key(seed), 5)
    return {
        "offsets": jnp.clip(1.0 * jax.random.uniform(keys[0], (3, CELLS_X, CELLS_Y, CELLS_Z, TILE), jnp.float32) ** block_scale(keys[0], (3, CELLS_X, CELLS_Y, CELLS_Z, TILE), ((1, 4), (2, 4), (3, 2)), -0.2, 0.2), 0.0, 1.0),
        "charge": bell_draw(keys[1], (CELLS_X, CELLS_Y, CELLS_Z, TILE), 0.5, 3.0, ((0, 4), (1, 4), (2, 2)), jnp.float32),
        "counts": draw_counts(jax.random.fold_in(keys[4], 71), 0),
        "partners": set_ends(jax.random.randint(keys[3], (CELLS_X, CELLS_Y, CELLS_Z, TILE), 0, TILE), jax.random.fold_in(keys[3], 1), 0, TILE - 1).astype(jnp.int32),
    }


highest = lax.Precision.HIGHEST
cutoff_sq = 64.0
soften_sq = 1.0
bond_spring = 0.1
fine_scale = 4.0
coarse_scale = 2.0
fine_spread = 2.5
coarse_spread = 6.0


def spline(shifted):
    magnitude = jnp.abs(shifted)
    margin = jnp.maximum(1.5 - magnitude, 0.0)
    return jnp.where(magnitude < 0.5, 0.75 - shifted * shifted, 0.5 * margin * margin)


def spline_slope(shifted):
    magnitude = jnp.abs(shifted)
    margin = jnp.maximum(1.5 - magnitude, 0.0)
    return jnp.where(magnitude < 0.5, -2.0 * shifted, jnp.where(shifted > 0.0, -margin, margin))


def patch_weights(offset):
    points = jnp.arange(11).astype(jnp.float32)
    shifted = 8.0 * offset[..., None] + 1.0 - points
    return spline(shifted), spline_slope(shifted)


def charge_patches(weighted, offsets):
    weight_x, _ = patch_weights(offsets[0])
    weight_y, _ = patch_weights(offsets[1])
    weight_z, _ = patch_weights(offsets[2])
    plane_part = weighted[..., None, None] * weight_x[..., :, None] * weight_y[..., None, :]
    flattened = plane_part.reshape(plane_part.shape[:-2] + (121,))
    joined = jnp.einsum("...sp,...sc->...pc", flattened, weight_z, precision=highest)
    return joined.reshape(joined.shape[:-2] + (11, 11, 11))


def assemble(values, where_axis):
    cell_count = values.shape[where_axis]
    inner_part = lax.slice_in_dim(values, 0, 8, axis=where_axis + 1)
    overflow = lax.slice_in_dim(values, 8, 11, axis=where_axis + 1)
    inner_pad = [(0, 0)] * values.ndim
    inner_pad[where_axis] = (0, 1)
    over_pad = [(0, 0)] * values.ndim
    over_pad[where_axis] = (1, 0)
    over_pad[where_axis + 1] = (0, 5)
    merged = jnp.pad(inner_part, inner_pad) + jnp.pad(overflow, over_pad)
    new_shape = values.shape[:where_axis] + (8 * (cell_count + 1),) + values.shape[where_axis + 2:]
    return merged.reshape(new_shape)


def cut_patches(values, where_axis):
    cell_count = (values.shape[where_axis] - 4) // 8
    split_shape = values.shape[:where_axis] + (cell_count, 8) + values.shape[where_axis + 1:]
    head_part = lax.slice_in_dim(values, 1, 8 * cell_count + 1, axis=where_axis).reshape(split_shape)
    widths = [(0, 0)] * values.ndim
    widths[where_axis] = (0, 5)
    padded = jnp.pad(values, widths)
    tail_part = lax.slice_in_dim(padded, 9, 8 * cell_count + 9, axis=where_axis).reshape(split_shape)
    tail_part = lax.slice_in_dim(tail_part, 0, 3, axis=where_axis + 1)
    return jnp.concatenate([head_part, tail_part], axis=where_axis + 1)


def kernel_band(in_length, spread):
    row_index = jnp.arange(in_length)[:, None]
    column_index = jnp.arange(in_length - 16)[None, :]
    distance = row_index - column_index - 8
    gap = distance.astype(jnp.float32)
    return jnp.where(jnp.abs(distance) <= 8, jnp.exp(-gap * gap / (2.0 * spread * spread)), 0.0).astype(jnp.float32)


def along_axis(values, matrix, where_axis):
    contracted = jnp.tensordot(values, matrix, axes=([where_axis], [0]), precision=highest)
    return jnp.moveaxis(contracted, -1, where_axis)


def convolve(values, spread, strength):
    for where_axis in range(3):
        values = along_axis(values, kernel_band(values.shape[where_axis], spread), where_axis)
    return strength * values


def grid_map(fine_length, coarse_length, fine_start, coarse_start):
    fine_index = jnp.arange(fine_length)[:, None] + fine_start
    coarse_index = jnp.arange(coarse_length)[None, :] + coarse_start
    gap = fine_index - 2 * coarse_index
    return jnp.where(gap == 0, 1.0, jnp.where(jnp.abs(gap) == 1, 0.5, 0.0)).astype(jnp.float32)


def cell_positions(offsets, first_cell):
    coordinates = []
    for dimension in range(3):
        cell_count = offsets.shape[dimension + 1]
        cell_index = jnp.arange(cell_count).astype(jnp.float32) + first_cell
        broadcast_shape = [1, 1, 1, 1]
        broadcast_shape[dimension] = cell_count
        coordinates.append((cell_index.reshape(broadcast_shape) + offsets[dimension]) * 8.0)
    return jnp.stack(coordinates)


def pair_sum(own_pos, own_charge, near_pos, near_charge):
    separation = own_pos[..., :, None] - near_pos[..., None, :]
    distance_sq = jnp.sum(separation * separation, axis=0)
    reach_left = jnp.maximum(1.0 - distance_sq / cutoff_sq, 0.0)
    strength = reach_left * reach_left * reach_left / (distance_sq + soften_sq) * near_charge[..., None, :]
    return own_charge * jnp.sum(separation * strength, axis=-1)


def bond_force(positions, in_use, partners):
    slot_ids = jnp.arange(positions.shape[-1]).astype(jnp.int32)
    picker = (partners[..., :, None] == slot_ids).astype(jnp.float32)
    partner_pos = jnp.einsum("...sp,d...p->d...s", picker, positions, precision=highest)
    partner_use = jnp.einsum("...sp,...p->...s", picker, in_use, precision=highest)
    return -bond_spring * (positions - partner_pos) * (in_use * partner_use)


def grid_force(patches, weighted, offsets):
    weight_x, slope_x = patch_weights(offsets[0])
    weight_y, slope_y = patch_weights(offsets[1])
    weight_z, slope_z = patch_weights(offsets[2])
    flattened = patches.reshape(patches.shape[:-3] + (121, 11))
    level_part = jnp.einsum("...pc,...sc->...sp", flattened, weight_z, precision=highest)
    rising = jnp.einsum("...pc,...sc->...sp", flattened, slope_z, precision=highest)
    level_part = level_part.reshape(level_part.shape[:-1] + (11, 11))
    rising = rising.reshape(rising.shape[:-1] + (11, 11))
    force_x = jnp.sum(slope_x[..., :, None] * weight_y[..., None, :] * level_part, axis=(-2, -1))
    force_y = jnp.sum(weight_x[..., :, None] * slope_y[..., None, :] * level_part, axis=(-2, -1))
    force_z = jnp.sum(weight_x[..., :, None] * weight_y[..., None, :] * rising, axis=(-2, -1))
    return -weighted * jnp.stack([force_x, force_y, force_z])


def reference(offsets, charge, counts, partners):
    slot_count = charge.shape[-1]
    cells_x, cells_y, cells_z = charge.shape[:3]
    in_use = (jnp.arange(slot_count).astype(jnp.int32) < counts[..., None]).astype(jnp.float32)
    weighted = charge * in_use
    positions = cell_positions(offsets, 0.0)
    padded_pos = cell_positions(jnp.pad(offsets, ((0, 0), (1, 1), (1, 1), (1, 1), (0, 0))), -1.0)
    padded_charge = jnp.pad(weighted, ((1, 1), (1, 1), (1, 1), (0, 0)))

    def pair_slab(slab_index):
        own_pos = lax.dynamic_index_in_dim(positions, slab_index, axis=1, keepdims=False)
        own_charge = lax.dynamic_index_in_dim(weighted, slab_index, axis=0, keepdims=False)
        own_use = lax.dynamic_index_in_dim(in_use, slab_index, axis=0, keepdims=False)
        own_partners = lax.dynamic_index_in_dim(partners, slab_index, axis=0, keepdims=False)
        running = bond_force(own_pos, own_use, own_partners)
        for step_x in range(3):
            slab_pos = lax.dynamic_index_in_dim(padded_pos, slab_index + step_x, axis=1, keepdims=False)
            slab_charge = lax.dynamic_index_in_dim(padded_charge, slab_index + step_x, axis=0, keepdims=False)
            for step_y in range(3):
                for step_z in range(3):
                    near_pos = slab_pos[:, step_y:step_y + cells_y, step_z:step_z + cells_z]
                    near_charge = slab_charge[step_y:step_y + cells_y, step_z:step_z + cells_z]
                    running = running + pair_sum(own_pos, own_charge, near_pos, near_charge)
        return running

    slab_ids = jnp.arange(cells_x).astype(jnp.int32)
    short_force = jnp.moveaxis(lax.map(pair_slab, slab_ids), 0, 1)

    offsets_slabs = jnp.moveaxis(offsets, 1, 0)

    def patch_slab(pieces_in):
        return charge_patches(pieces_in[0], pieces_in[1])

    patches = lax.map(patch_slab, (weighted, offsets_slabs))
    spread_grid = jnp.transpose(patches, (0, 3, 1, 4, 2, 5))
    for where_axis in range(3):
        spread_grid = assemble(spread_grid, where_axis)
    grid_x, grid_y, grid_z = 8 * cells_x, 8 * cells_y, 8 * cells_z
    fine_charge = spread_grid[1:grid_x + 1, 1:grid_y + 1, 1:grid_z + 1]
    fine_potential = convolve(jnp.pad(fine_charge, 8), fine_spread, fine_scale)
    coarse_maps = [grid_map(length, length // 2, 0, 0) for length in (grid_x, grid_y, grid_z)]
    coarse_charge = fine_charge
    for where_axis in range(3):
        coarse_charge = along_axis(coarse_charge, coarse_maps[where_axis], where_axis)
    coarse_potential = convolve(jnp.pad(coarse_charge, 8), coarse_spread, coarse_scale)
    potential = coarse_potential
    for where_axis in range(3):
        potential = along_axis(potential, jnp.transpose(coarse_maps[where_axis]), where_axis)
    potential = jnp.pad(fine_potential + potential, 2)
    for where_axis in range(3):
        potential = cut_patches(potential, 2 * where_axis)
    near_grid = jnp.transpose(potential, (0, 2, 4, 1, 3, 5))

    def force_slab(pieces_in):
        return grid_force(pieces_in[0], pieces_in[1], pieces_in[2])

    long_force = jnp.moveaxis(lax.map(force_slab, (near_grid, weighted, offsets_slabs)), 0, 1)
    return short_force, long_force
```

```python
import jax
import jax.numpy as jnp
from jax import lax
from jax.experimental import pallas as pl
from jax.experimental.pallas import tpu as pltpu
from jax.sharding import PartitionSpec as P

highest = lax.Precision.HIGHEST
bond_spring = 0.1
fine_scale = 4.0
coarse_scale = 2.0
fine_spread = 2.5
coarse_spread = 6.0


def padded_2(value, sides, width):
    for axis, dim in sides:
        size, length = (lax.axis_size(axis), value.shape[dim])
        up = [(i, (i + 1) % size) for i in range(size - 1)]
        down = [(j, i) for i, j in up]
        last = lax.slice_in_dim(value, length - width, length, axis=dim)
        initial = lax.slice_in_dim(value, 0, width, axis=dim)
        before = lax.ppermute(last, axis, up)
        after = lax.ppermute(initial, axis, down)
        value = jnp.concatenate([before, value, after], axis=dim)
    return value


def spline(shifted):
    magnitude = jnp.abs(shifted)
    margin = jnp.maximum(1.5 - magnitude, 0.0)
    return jnp.where(magnitude < 0.5, 0.75 - shifted * shifted, 0.5 * margin * margin)


def spline_slope(shifted):
    magnitude = jnp.abs(shifted)
    margin = jnp.maximum(1.5 - magnitude, 0.0)
    return jnp.where(magnitude < 0.5, -2.0 * shifted, jnp.where(shifted > 0.0, -margin, margin))


def patch_weights(offset):
    points = jnp.arange(11).astype(jnp.float32)
    shifted = 8.0 * offset[..., None] + 1.0 - points
    return (spline(shifted), spline_slope(shifted))


def charge_patches(weighted, offsets):
    weight_x, _ = patch_weights(offsets[0])
    weight_y, _ = patch_weights(offsets[1])
    weight_z, _ = patch_weights(offsets[2])
    plane_part = weighted[..., None, None] * weight_x[..., :, None] * weight_y[..., None, :]
    flattened = plane_part.reshape(plane_part.shape[:-2] + (121,))
    joined = jnp.einsum("...sp,...sc->...pc", flattened, weight_z, precision=highest)
    return joined.reshape(joined.shape[:-2] + (11, 11, 11))


def assemble(values, where_axis):
    cell_count = values.shape[where_axis]
    inner_part = lax.slice_in_dim(values, 0, 8, axis=where_axis + 1)
    overflow = lax.slice_in_dim(values, 8, 11, axis=where_axis + 1)
    inner_pad = [(0, 0)] * values.ndim
    inner_pad[where_axis] = (0, 1)
    over_pad = [(0, 0)] * values.ndim
    over_pad[where_axis] = (1, 0)
    over_pad[where_axis + 1] = (0, 5)
    merged = jnp.pad(inner_part, inner_pad) + jnp.pad(overflow, over_pad)
    new_shape = values.shape[:where_axis] + (8 * (cell_count + 1),) + values.shape[where_axis + 2 :]
    return merged.reshape(new_shape)


def cut_patches(values, where_axis):
    cell_count = (values.shape[where_axis] - 4) // 8
    split_shape = values.shape[:where_axis] + (cell_count, 8) + values.shape[where_axis + 1 :]
    head_part = lax.slice_in_dim(values, 1, 8 * cell_count + 1, axis=where_axis).reshape(
        split_shape
    )
    widths = [(0, 0)] * values.ndim
    widths[where_axis] = (0, 5)
    padded = jnp.pad(values, widths)
    tail_part = lax.slice_in_dim(padded, 9, 8 * cell_count + 9, axis=where_axis).reshape(
        split_shape
    )
    tail_part = lax.slice_in_dim(tail_part, 0, 3, axis=where_axis + 1)
    return jnp.concatenate([head_part, tail_part], axis=where_axis + 1)


def kernel_band(in_length, spread):
    row_index = jnp.arange(in_length)[:, None]
    column_index = jnp.arange(in_length - 16)[None, :]
    distance = row_index - column_index - 8
    gap = distance.astype(jnp.float32)
    return jnp.where(jnp.abs(distance) <= 8, jnp.exp(-gap * gap / (2.0 * spread * spread)), 0.0)


def along_axis(values, matrix, where_axis):
    contracted = jnp.tensordot(values, matrix, axes=([where_axis], [0]), precision=highest)
    return jnp.moveaxis(contracted, -1, where_axis)


def convolve(values, spread, strength):
    for where_axis in range(3):
        values = along_axis(values, kernel_band(values.shape[where_axis], spread), where_axis)
    return strength * values


def grid_map(fine_length, coarse_length, fine_start, coarse_start):
    fine_index = jnp.arange(fine_length)[:, None] + fine_start
    coarse_index = jnp.arange(coarse_length)[None, :] + coarse_start
    gap = fine_index - 2 * coarse_index
    return jnp.where(gap == 0, 1.0, jnp.where(jnp.abs(gap) == 1, 0.5, 0.0)).astype(jnp.float32)


def cell_positions(offsets, first_cell):
    coordinates = []
    for dimension in range(3):
        cell_count = offsets.shape[dimension + 1]
        cell_index = jnp.arange(cell_count).astype(jnp.float32) + first_cell
        broadcast_shape = [1, 1, 1, 1]
        broadcast_shape[dimension] = cell_count
        coordinates.append((cell_index.reshape(broadcast_shape) + offsets[dimension]))
    return jnp.stack(coordinates)


def short_kernel(counts_ref, grown_ref, partners_ref, out_ref, own_s, acc_s):
    _, cells_x, cells_y, cells_z, slots = out_ref.shape
    lane = lax.broadcasted_iota(jnp.int32, (1, slots), 1)

    def cell_body(cell, carry):
        i = cell // (cells_y * cells_z)
        j = (cell // cells_z) % cells_y
        k = cell % cells_z
        count = counts_ref[cell]
        own_rows = [grown_ref[d, i + 1, j + 1, pl.ds(k + 1, 1), :] for d in range(3)]
        for d in range(3):
            own_s[d] = jnp.broadcast_to(own_rows[d], (slots, slots)).T

        def block_body(block, carry):
            row = pl.multiple_of(block * 8, 8)
            own = [own_s[d, pl.ds(row, 8), :] for d in range(3)]
            total = [jnp.zeros((8, slots), jnp.float32) for _ in range(3)]
            for step_x in range(3):
                for step_y in range(3):
                    for step_z in range(3):
                        near = [
                            grown_ref[d, i + step_x, j + step_y, pl.ds(k + step_z, 1), :]
                            for d in range(4)
                        ]
                        gap = [own[d] - near[d] for d in range(3)]
                        distance_sq = gap[0] * gap[0] + gap[1] * gap[1] + gap[2] * gap[2]
                        reach = jnp.maximum(1.0 - distance_sq, 0.0)
                        below = 1.015625 - reach
                        inverse = pl.reciprocal(below, approx=True)
                        inverse = inverse * (2.0 - below * inverse)
                        strength = (reach * reach) * (reach * near[3]) * inverse
                        total = [total[d] + strength * gap[d] for d in range(3)]
            for d in range(3):
                acc_s[d, pl.ds(row, 8), :] = total[d]
            return carry

        lax.fori_loop(0, (count + 7) // 8, block_body, 0)
        charge = grown_ref[3, i + 1, j + 1, pl.ds(k + 1, 1), :]
        partner = partners_ref[i, j, pl.ds(k, 1), :]
        bonded = (lane < count) & (partner < count)
        index = jnp.broadcast_to(partner, (8, slots))
        for d in range(3):
            pair = 0.125 * charge * jnp.sum(acc_s[d].T, axis=0, keepdims=True)
            source = jnp.broadcast_to(own_rows[d], (8, slots))
            other = jnp.take_along_axis(source, index, axis=1)[0:1]
            bond = jnp.where(bonded, (-8.0 * bond_spring) * (own_rows[d] - other), 0.0)
            out_ref[d, i, j, pl.ds(k, 1), :] = jnp.where(lane < count, pair, 0.0) + bond
        return carry

    lax.fori_loop(0, cells_x * cells_y * cells_z, cell_body, 0)


def short_forces(counts, grown, partners):
    cells, slots = counts.shape, partners.shape[-1]
    return pl.pallas_call(
        short_kernel,
        out_shape=jax.ShapeDtypeStruct((3,) + cells + (slots,), jnp.float32),
        in_specs=[pl.BlockSpec(memory_space=pltpu.SMEM)]
        + [pl.BlockSpec(memory_space=pltpu.VMEM)] * 2,
        out_specs=pl.BlockSpec(memory_space=pltpu.VMEM),
        scratch_shapes=[pltpu.VMEM((3, slots, slots), jnp.float32)] * 2,
        compiler_params=pltpu.CompilerParams(vmem_limit_bytes=24 * 2**20),
        cost_estimate=pl.CostEstimate(flops=10**9, bytes_accessed=10**7, transcendentals=10**7),
    )(counts.reshape(-1), grown, partners)


def grid_force(patches, weighted, offsets):
    weight_x, slope_x = patch_weights(offsets[0])
    weight_y, slope_y = patch_weights(offsets[1])
    weight_z, slope_z = patch_weights(offsets[2])
    flattened = patches.reshape(patches.shape[:-3] + (121, 11))
    level_part = jnp.einsum("...pc,...sc->...sp", flattened, weight_z, precision=highest)
    rising = jnp.einsum("...pc,...sc->...sp", flattened, slope_z, precision=highest)
    level_part = level_part.reshape(level_part.shape[:-1] + (11, 11))
    rising = rising.reshape(rising.shape[:-1] + (11, 11))
    force_x = jnp.sum(slope_x[..., :, None] * weight_y[..., None, :] * level_part, axis=(-2, -1))
    force_y = jnp.sum(weight_x[..., :, None] * slope_y[..., None, :] * level_part, axis=(-2, -1))
    force_z = jnp.sum(weight_x[..., :, None] * weight_y[..., None, :] * rising, axis=(-2, -1))
    return -weighted * jnp.stack([force_x, force_y, force_z])


def inside_grid(fine_length, first_point, device_count):
    coordinate = jnp.arange(fine_length + 4) - 2 + first_point
    return ((coordinate >= 0) & (coordinate < fine_length * device_count)).astype(jnp.float32)


def per_device(offsets, charge, counts, partners):
    slot_count = charge.shape[-1]
    cells_x, cells_y, cells_z = charge.shape[:3]
    in_use = (jnp.arange(slot_count) < counts[..., None]).astype(jnp.float32)
    weighted = charge * in_use
    packed = jnp.concatenate([offsets, weighted[None]], axis=0)
    grown_tiles = padded_2(packed, (("gx", 1), ("gy", 2), ("ga", 3)), 1)
    grown_offsets = grown_tiles[:3]
    grown_charge = grown_tiles[3]
    cell_units = cell_positions(grown_offsets, -1.0)
    grown = jnp.concatenate([cell_units, grown_charge[None]], axis=0)
    short_force = short_forces(counts, grown, partners)
    patches = charge_patches(grown_charge, grown_offsets)
    spread_grid = jnp.transpose(patches, (0, 3, 1, 4, 2, 5))
    for where_axis in range(3):
        spread_grid = assemble(spread_grid, where_axis)
    grid_x, grid_y, grid_z = (8 * cells_x, 8 * cells_y, 8 * cells_z)
    fine_charge = spread_grid[9 : 9 + grid_x, 9 : 9 + grid_y, 9 : 9 + grid_z]
    halo_depth = 10
    widened = padded_2(fine_charge, (("gx", 0), ("gy", 1), ("ga", 2)), halo_depth)
    fine_potential = convolve(widened, fine_spread, fine_scale)
    coarse_charge = widened
    for where_axis, fine_length in enumerate((grid_x, grid_y, grid_z)):
        coarse_charge = along_axis(
            coarse_charge,
            grid_map(fine_length + 2 * halo_depth, fine_length // 2, -halo_depth, 0),
            where_axis,
        )
    grown_coarse = padded_2(coarse_charge, (("gx", 0), ("gy", 1), ("ga", 2)), 8)
    coarse_potential = convolve(grown_coarse, coarse_spread, coarse_scale)
    coarse_near = padded_2(coarse_potential, (("gx", 0), ("gy", 1), ("ga", 2)), 2)
    potential = coarse_near
    for where_axis, fine_length in enumerate((grid_x, grid_y, grid_z)):
        potential = along_axis(
            potential,
            jnp.transpose(grid_map(fine_length + 4, fine_length // 2 + 4, -2, -2)),
            where_axis,
        )
    inside_x = inside_grid(grid_x, lax.axis_index("gx") * grid_x, lax.axis_size("gx"))
    inside_y = inside_grid(grid_y, lax.axis_index("gy") * grid_y, lax.axis_size("gy"))
    inside_z = inside_grid(grid_z, lax.axis_index("ga") * grid_z, lax.axis_size("ga"))
    inside_mask = inside_x[:, None, None] * inside_y[None, :, None] * inside_z[None, None, :]
    potential = (potential + fine_potential) * inside_mask
    for where_axis in range(3):
        potential = cut_patches(potential, 2 * where_axis)
    near_grid = jnp.transpose(potential, (0, 2, 4, 1, 3, 5))
    long_force = grid_force(near_grid, weighted, offsets)
    return (short_force, long_force)


def solution(mesh):
    return jax.shard_map(
        per_device,
        mesh=mesh,
        in_specs=(
            P(None, "gx", "gy", "ga", None),
            P("gx", "gy", "ga", None),
            P("gx", "gy", "ga"),
            P("gx", "gy", "ga", None),
        ),
        out_specs=(P(None, "gx", "gy", "ga", None), P(None, "gx", "gy", "ga", None)),
        check_vma=False,
    )
```

```python
import jax
import jax.numpy as jnp
from jax import lax
from jax.experimental import pallas as pl
from jax.experimental.pallas import tpu as pltpu
from jax.sharding import PartitionSpec as P

highest = lax.Precision.HIGHEST
bond_spring = 0.1
fine_scale = 4.0
coarse_scale = 2.0
fine_spread = 2.5
coarse_spread = 6.0


def padded_2(value, sides, width):
    for axis, dim in sides:
        size, length = (lax.axis_size(axis), value.shape[dim])
        up = [(i, (i + 1) % size) for i in range(size - 1)]
        down = [(j, i) for i, j in up]
        last = lax.slice_in_dim(value, length - width, length, axis=dim)
        initial = lax.slice_in_dim(value, 0, width, axis=dim)
        before = lax.ppermute(last, axis, up)
        after = lax.ppermute(initial, axis, down)
        value = jnp.concatenate([before, value, after], axis=dim)
    return value


def spline(shifted):
    magnitude = jnp.abs(shifted)
    margin = jnp.maximum(1.5 - magnitude, 0.0)
    return jnp.where(magnitude < 0.5, 0.75 - shifted * shifted, 0.5 * margin * margin)


def spline_slope(shifted):
    magnitude = jnp.abs(shifted)
    margin = jnp.maximum(1.5 - magnitude, 0.0)
    return jnp.where(magnitude < 0.5, -2.0 * shifted, jnp.where(shifted > 0.0, -margin, margin))


def split_product(left, right, dims):
    left_high, right_high = left.astype(jnp.bfloat16), right.astype(jnp.bfloat16)
    left_low = (left - left_high.astype(jnp.float32)).astype(jnp.bfloat16)
    right_low = (right - right_high.astype(jnp.float32)).astype(jnp.bfloat16)

    def product(one, other):
        return lax.dot_general(one, other, (dims, ((), ())), preferred_element_type=jnp.float32)

    return product(left_high, right_high) + (
        product(left_low, right_high) + product(left_high, right_low)
    )


def row_of_cells(ref, lead, k):
    return jnp.concatenate([ref[lead + (j, pl.ds(k, 1))] for j in range(ref.shape[-3])], axis=1)


def point_gaps(offset, count, shift):
    points = lax.broadcasted_iota(jnp.int32, (count, offset.shape[1]), 0).astype(jnp.float32)
    return (8.0 * offset + 1.0 + shift) - points


def cell_shift(cells_y, slots):
    lane = lax.broadcasted_iota(jnp.int32, (1, cells_y * slots), 1)
    return 8.0 * (lane // slots).astype(jnp.float32)


def spread_kernel(offsets_ref, weighted_ref, grid_ref):
    cells_x, cells_y, cells_z, slots = weighted_ref.shape
    width = grid_ref.shape[-1]
    grid_ref[...] = jnp.zeros_like(grid_ref)
    shift_y = cell_shift(cells_y, slots)

    def body(step, carry):
        i, k = step // cells_z, step % cells_z
        off_x, off_y, off_z = [row_of_cells(offsets_ref, (d, i), k) for d in range(3)]
        charge = row_of_cells(weighted_ref, (i,), k)
        weight_x = spline(point_gaps(off_x, 16, 0.0)) * charge
        weight_z = spline(point_gaps(off_z, 16, 0.0))
        weight_y = spline(point_gaps(off_y, width, shift_y))
        plane = jnp.concatenate([weight_x[a : a + 1] * weight_z for a in range(11)], axis=0)
        patch = split_product(plane, weight_y, ((1,), (1,)))
        for a in range(11):
            rows = pl.ds(pl.multiple_of(8 * k, 8), 16)
            grid_ref[8 * i + a, rows, :] += patch[16 * a : 16 * a + 16]
        return carry

    lax.fori_loop(0, cells_x * cells_z, body, 0)


def spread_charge(offsets, weighted):
    cells_x, cells_y, cells_z, _ = weighted.shape
    width = 8 * cells_y + 16
    grid = pl.pallas_call(
        spread_kernel,
        out_shape=jax.ShapeDtypeStruct((8 * cells_x + 3, 8 * cells_z + 8, width), jnp.float32),
        in_specs=[pl.BlockSpec(memory_space=pltpu.VMEM)] * 2,
        out_specs=pl.BlockSpec(memory_space=pltpu.VMEM),
        compiler_params=pltpu.CompilerParams(vmem_limit_bytes=24 * 2**20),
        cost_estimate=pl.CostEstimate(flops=10**8, bytes_accessed=4 * 10**6, transcendentals=0),
    )(offsets, weighted)
    return jnp.transpose(grid[:, : 8 * cells_z + 3, : 8 * cells_y + 3], (0, 2, 1))


def gather_kernel(offsets_ref, weighted_ref, grid_ref, out_ref):
    cells_x, cells_y, cells_z, slots = weighted_ref.shape
    width = grid_ref.shape[-1] // 3
    shift_y = cell_shift(cells_y, slots)
    lane = lax.broadcasted_iota(jnp.int32, (16, 3 * width), 1)
    middle = (lane >= width) & (lane < 2 * width)

    def body(step, carry):
        i, k = step // cells_z, step % cells_z
        off_x, off_y, off_z = [row_of_cells(offsets_ref, (d, i), k) for d in range(3)]
        gap_x, gap_z = point_gaps(off_x, 16, 0.0), point_gaps(off_z, 16, 0.0)
        gap_y = point_gaps(off_y, width, shift_y)
        weight_x, slope_x = spline(gap_x), spline_slope(gap_x)
        weight_z, slope_z = spline(gap_z), spline_slope(gap_z)
        both_y = jnp.concatenate([spline(gap_y), spline_slope(gap_y)], axis=1)
        y_high = both_y.astype(jnp.bfloat16)
        y_low = (both_y - y_high.astype(jnp.float32)).astype(jnp.bfloat16)
        parts = []
        for a in range(11):
            part = grid_ref[8 * i + a, pl.ds(pl.multiple_of(8 * k, 8), 16), :]
            low = part - part.astype(jnp.bfloat16).astype(jnp.float32)
            parts.append(jnp.where(middle, low, part).astype(jnp.bfloat16))
        found = jnp.dot(
            jnp.concatenate(parts, axis=0),
            jnp.concatenate([y_high, y_high, y_low], axis=0),
            preferred_element_type=jnp.float32,
        )
        lanes = cells_y * slots
        totals = [jnp.zeros((16, lanes), jnp.float32) for _ in range(3)]
        for a in range(11):
            level = found[16 * a : 16 * a + 16, :lanes]
            rising = found[16 * a : 16 * a + 16, lanes:]
            totals[0] += slope_x[a : a + 1] * level
            totals[1] += weight_x[a : a + 1] * rising
            totals[2] += weight_x[a : a + 1] * level
        charge = row_of_cells(weighted_ref, (i,), k)
        for d, along_z in enumerate((weight_z, weight_z, slope_z)):
            force = -charge * jnp.sum(totals[d] * along_z, axis=0, keepdims=True)
            for j in range(cells_y):
                out_ref[d, i, j, pl.ds(k, 1), :] = force[:, j * slots : (j + 1) * slots]
        return carry

    lax.fori_loop(0, cells_x * cells_z, body, 0)


def grid_forces(offsets, weighted, potential):
    cells_x, cells_y, cells_z, _ = weighted.shape
    width = 8 * cells_y + 16
    grid = jnp.transpose(potential[1:, 1:, 1:], (0, 2, 1))
    grid = jnp.pad(grid, ((0, 0), (0, 8 * cells_z + 8 - grid.shape[1]), (0, width - grid.shape[2])))
    grid = jnp.concatenate([grid] * 3, axis=2)
    return pl.pallas_call(
        gather_kernel,
        out_shape=jax.ShapeDtypeStruct(offsets.shape, jnp.float32),
        in_specs=[pl.BlockSpec(memory_space=pltpu.VMEM)] * 3,
        out_specs=pl.BlockSpec(memory_space=pltpu.VMEM),
        compiler_params=pltpu.CompilerParams(vmem_limit_bytes=24 * 2**20),
        cost_estimate=pl.CostEstimate(flops=10**8, bytes_accessed=4 * 10**6, transcendentals=0),
    )(offsets, weighted, grid)


def spread_halo(value, sides, depth):
    for axis, dim in sides:
        size, length = (lax.axis_size(axis), value.shape[dim] - 3)
        up = [(i, (i + 1) % size) for i in range(size - 1)]
        down = [(j, i) for i, j in up]
        last = lax.slice_in_dim(value, length - depth + 1, length + 3, axis=dim)
        initial = lax.slice_in_dim(value, 0, depth + 1, axis=dim)
        before = lax.ppermute(last, axis, up)
        after = lax.ppermute(initial, axis, down)

        def placed(part, low, high):
            widths = [(0, 0)] * part.ndim
            widths[dim] = (low, high)
            return jnp.pad(part, widths)

        value = (
            placed(value, depth - 1, depth - 2)
            + placed(before, 0, length + depth - 2)
            + placed(after, length + depth - 1, 0)
        )
    return value


def kernel_band(in_length, spread):
    row_index = jnp.arange(in_length)[:, None]
    column_index = jnp.arange(in_length - 16)[None, :]
    distance = row_index - column_index - 8
    gap = distance.astype(jnp.float32)
    return jnp.where(jnp.abs(distance) <= 8, jnp.exp(-gap * gap / (2.0 * spread * spread)), 0.0)


def along_axis(values, matrix, where_axis):
    contracted = jnp.tensordot(values, matrix, axes=([where_axis], [0]), precision=highest)
    return jnp.moveaxis(contracted, -1, where_axis)


def convolve(values, spread, strength):
    for where_axis in range(3):
        values = along_axis(values, kernel_band(values.shape[where_axis], spread), where_axis)
    return strength * values


def grid_map(fine_length, coarse_length, fine_start, coarse_start):
    fine_index = jnp.arange(fine_length)[:, None] + fine_start
    coarse_index = jnp.arange(coarse_length)[None, :] + coarse_start
    gap = fine_index - 2 * coarse_index
    return jnp.where(gap == 0, 1.0, jnp.where(jnp.abs(gap) == 1, 0.5, 0.0)).astype(jnp.float32)


def cell_positions(offsets, first_cell):
    coordinates = []
    for dimension in range(3):
        cell_count = offsets.shape[dimension + 1]
        cell_index = jnp.arange(cell_count).astype(jnp.float32) + first_cell
        broadcast_shape = [1, 1, 1, 1]
        broadcast_shape[dimension] = cell_count
        coordinates.append((cell_index.reshape(broadcast_shape) + offsets[dimension]))
    return jnp.stack(coordinates)


def short_kernel(counts_ref, grown_ref, partners_ref, out_ref, own_s, acc_s):
    _, cells_x, cells_y, cells_z, slots = out_ref.shape
    lane = lax.broadcasted_iota(jnp.int32, (1, slots), 1)

    def cell_body(cell, carry):
        i = cell // (cells_y * cells_z)
        j = (cell // cells_z) % cells_y
        k = cell % cells_z
        count = counts_ref[cell]
        own_rows = [grown_ref[d, i + 1, j + 1, pl.ds(k + 1, 1), :] for d in range(3)]
        for d in range(3):
            own_s[d] = jnp.broadcast_to(own_rows[d], (slots, slots)).T

        def block_body(block, carry):
            row = pl.multiple_of(block * 8, 8)
            own = [own_s[d, pl.ds(row, 8), :] for d in range(3)]
            total = [jnp.zeros((8, slots), jnp.float32) for _ in range(3)]
            for step_x in range(3):
                for step_y in range(3):
                    for step_z in range(3):
                        near = [
                            grown_ref[d, i + step_x, j + step_y, pl.ds(k + step_z, 1), :]
                            for d in range(4)
                        ]
                        gap = [own[d] - near[d] for d in range(3)]
                        distance_sq = gap[0] * gap[0] + gap[1] * gap[1] + gap[2] * gap[2]
                        reach = jnp.maximum(1.0 - distance_sq, 0.0)
                        below = 1.015625 - reach
                        inverse = pl.reciprocal(below, approx=True)
                        inverse = inverse * (2.0 - below * inverse)
                        strength = (reach * reach) * (reach * near[3]) * inverse
                        total = [total[d] + strength * gap[d] for d in range(3)]
            for d in range(3):
                acc_s[d, pl.ds(row, 8), :] = total[d]
            return carry

        lax.fori_loop(0, (count + 7) // 8, block_body, 0)
        charge = grown_ref[3, i + 1, j + 1, pl.ds(k + 1, 1), :]
        partner = partners_ref[i, j, pl.ds(k, 1), :]
        bonded = (lane < count) & (partner < count)
        index = jnp.broadcast_to(partner, (8, slots))
        for d in range(3):
            pair = 0.125 * charge * jnp.sum(acc_s[d].T, axis=0, keepdims=True)
            source = jnp.broadcast_to(own_rows[d], (8, slots))
            other = jnp.take_along_axis(source, index, axis=1)[0:1]
            bond = jnp.where(bonded, (-8.0 * bond_spring) * (own_rows[d] - other), 0.0)
            out_ref[d, i, j, pl.ds(k, 1), :] = jnp.where(lane < count, pair, 0.0) + bond
        return carry

    lax.fori_loop(0, cells_x * cells_y * cells_z, cell_body, 0)


def short_forces(counts, grown, partners):
    cells, slots = counts.shape, partners.shape[-1]
    return pl.pallas_call(
        short_kernel,
        out_shape=jax.ShapeDtypeStruct((3,) + cells + (slots,), jnp.float32),
        in_specs=[pl.BlockSpec(memory_space=pltpu.SMEM)]
        + [pl.BlockSpec(memory_space=pltpu.VMEM)] * 2,
        out_specs=pl.BlockSpec(memory_space=pltpu.VMEM),
        scratch_shapes=[pltpu.VMEM((3, slots, slots), jnp.float32)] * 2,
        compiler_params=pltpu.CompilerParams(vmem_limit_bytes=24 * 2**20),
        cost_estimate=pl.CostEstimate(flops=10**9, bytes_accessed=10**7, transcendentals=10**7),
    )(counts.reshape(-1), grown, partners)


def inside_mask(lengths, depth):
    mask = jnp.float32(1.0)
    for dim, axis in enumerate(("gx", "gy", "ga")):
        length = lengths[dim]
        first = lax.axis_index(axis) * length - depth
        point = jnp.arange(length + 2 * depth) + first
        inside = (point >= 0) & (point < length * lax.axis_size(axis))
        shape = [1, 1, 1]
        shape[dim] = length + 2 * depth
        mask = mask * inside.astype(jnp.float32).reshape(shape)
    return mask


def per_device(offsets, charge, counts, partners):
    slot_count = charge.shape[-1]
    cells_x, cells_y, cells_z = charge.shape[:3]
    in_use = (jnp.arange(slot_count) < counts[..., None]).astype(jnp.float32)
    weighted = charge * in_use
    packed = jnp.concatenate([offsets, weighted[None]], axis=0)
    grown_tiles = padded_2(packed, (("gx", 1), ("gy", 2), ("ga", 3)), 1)
    grown_offsets = grown_tiles[:3]
    grown_charge = grown_tiles[3]
    cell_units = cell_positions(grown_offsets, -1.0)
    grown = jnp.concatenate([cell_units, grown_charge[None]], axis=0)
    short_force = short_forces(counts, grown, partners)
    grid_x, grid_y, grid_z = (8 * cells_x, 8 * cells_y, 8 * cells_z)
    lengths = (grid_x, grid_y, grid_z)
    halo_depth = 10
    spread = spread_charge(offsets, weighted)
    widened = spread_halo(spread, (("gx", 0), ("gy", 1), ("ga", 2)), halo_depth)
    widened = widened * inside_mask(lengths, halo_depth)
    fine_potential = convolve(widened, fine_spread, fine_scale)
    coarse_charge = widened
    for where_axis, fine_length in enumerate((grid_x, grid_y, grid_z)):
        coarse_charge = along_axis(
            coarse_charge,
            grid_map(fine_length + 2 * halo_depth, fine_length // 2, -halo_depth, 0),
            where_axis,
        )
    grown_coarse = padded_2(coarse_charge, (("gx", 0), ("gy", 1), ("ga", 2)), 8)
    coarse_potential = convolve(grown_coarse, coarse_spread, coarse_scale)
    coarse_near = padded_2(coarse_potential, (("gx", 0), ("gy", 1), ("ga", 2)), 2)
    potential = coarse_near
    for where_axis, fine_length in enumerate((grid_x, grid_y, grid_z)):
        potential = along_axis(
            potential,
            jnp.transpose(grid_map(fine_length + 4, fine_length // 2 + 4, -2, -2)),
            where_axis,
        )
    potential = (potential + fine_potential) * inside_mask(lengths, 2)
    long_force = grid_forces(offsets, weighted, potential)
    return (short_force, long_force)


def solution(mesh):
    return jax.shard_map(
        per_device,
        mesh=mesh,
        in_specs=(
            P(None, "gx", "gy", "ga", None),
            P("gx", "gy", "ga", None),
            P("gx", "gy", "ga"),
            P("gx", "gy", "ga", None),
        ),
        out_specs=(P(None, "gx", "gy", "ga", None), P(None, "gx", "gy", "ga", None)),
        check_vma=False,
    )
```

```python
import jax
import jax.numpy as jnp
from jax import lax
from jax.experimental import pallas as pl
from jax.experimental.pallas import tpu as pltpu
from jax.sharding import PartitionSpec as P

highest = lax.Precision.HIGHEST
bond_spring = 0.1
fine_scale = 4.0
coarse_scale = 2.0
fine_spread = 2.5
coarse_spread = 6.0


def padded_2(value, sides, width):
    for axis, dim in sides:
        size, length = (lax.axis_size(axis), value.shape[dim])
        up = [(i, (i + 1) % size) for i in range(size - 1)]
        down = [(j, i) for i, j in up]
        last = lax.slice_in_dim(value, length - width, length, axis=dim)
        initial = lax.slice_in_dim(value, 0, width, axis=dim)
        before = lax.ppermute(last, axis, up)
        after = lax.ppermute(initial, axis, down)
        value = jnp.concatenate([before, value, after], axis=dim)
    return value


def spline(shifted):
    magnitude = jnp.abs(shifted)
    margin = jnp.maximum(1.5 - magnitude, 0.0)
    return jnp.where(magnitude < 0.5, 0.75 - shifted * shifted, 0.5 * margin * margin)


def spline_slope(shifted):
    magnitude = jnp.abs(shifted)
    margin = jnp.maximum(1.5 - magnitude, 0.0)
    return jnp.where(magnitude < 0.5, -2.0 * shifted, jnp.where(shifted > 0.0, -margin, margin))


def split_product(left, right, dims):
    left_high, right_high = left.astype(jnp.bfloat16), right.astype(jnp.bfloat16)
    left_low = (left - left_high.astype(jnp.float32)).astype(jnp.bfloat16)
    right_low = (right - right_high.astype(jnp.float32)).astype(jnp.bfloat16)

    def product(one, other):
        return lax.dot_general(one, other, (dims, ((), ())), preferred_element_type=jnp.float32)

    return product(left_high, right_high) + (
        product(left_low, right_high) + product(left_high, right_low)
    )


def row_of_cells(ref, lead, k):
    return jnp.concatenate([ref[lead + (j, pl.ds(k, 1))] for j in range(ref.shape[-3])], axis=1)


def point_gaps(offset, count, shift):
    points = lax.broadcasted_iota(jnp.int32, (count, offset.shape[1]), 0).astype(jnp.float32)
    return (8.0 * offset + 1.0 + shift) - points


def cell_shift(cells_y, slots):
    lane = lax.broadcasted_iota(jnp.int32, (1, cells_y * slots), 1)
    return 8.0 * (lane // slots).astype(jnp.float32)


def spread_kernel(offsets_ref, weighted_ref, grid_ref):
    cells_x, cells_y, cells_z, slots = weighted_ref.shape
    width = grid_ref.shape[-1]
    grid_ref[...] = jnp.zeros_like(grid_ref)
    shift_y = cell_shift(cells_y, slots)

    def body(step, carry):
        i, k = step // cells_z, step % cells_z
        off_x, off_y, off_z = [row_of_cells(offsets_ref, (d, i), k) for d in range(3)]
        charge = row_of_cells(weighted_ref, (i,), k)
        weight_x = spline(point_gaps(off_x, 16, 0.0)) * charge
        weight_z = spline(point_gaps(off_z, 16, 0.0))
        weight_y = spline(point_gaps(off_y, width, shift_y))
        plane = jnp.concatenate([weight_x[a : a + 1] * weight_z for a in range(11)], axis=0)
        patch = split_product(plane, weight_y, ((1,), (1,)))
        for a in range(11):
            rows = pl.ds(pl.multiple_of(8 * k, 8), 16)
            grid_ref[8 * i + a, rows, :] += patch[16 * a : 16 * a + 16]
        return carry

    lax.fori_loop(0, cells_x * cells_z, body, 0)


def spread_charge(offsets, weighted):
    cells_x, cells_y, cells_z, _ = weighted.shape
    width = 8 * cells_y + 16
    grid = pl.pallas_call(
        spread_kernel,
        out_shape=jax.ShapeDtypeStruct((8 * cells_x + 3, 8 * cells_z + 8, width), jnp.float32),
        in_specs=[pl.BlockSpec(memory_space=pltpu.VMEM)] * 2,
        out_specs=pl.BlockSpec(memory_space=pltpu.VMEM),
        compiler_params=pltpu.CompilerParams(vmem_limit_bytes=24 * 2**20),
        cost_estimate=pl.CostEstimate(flops=10**8, bytes_accessed=4 * 10**6, transcendentals=0),
    )(offsets, weighted)
    return jnp.transpose(grid[:, : 8 * cells_z + 3, : 8 * cells_y + 3], (0, 2, 1))


def gather_kernel(offsets_ref, weighted_ref, grid_ref, out_ref):
    cells_x, cells_y, cells_z, slots = weighted_ref.shape
    width = grid_ref.shape[-1] // 3
    shift_y = cell_shift(cells_y, slots)
    lane = lax.broadcasted_iota(jnp.int32, (16, 3 * width), 1)
    middle = (lane >= width) & (lane < 2 * width)

    def body(step, carry):
        i, k = step // cells_z, step % cells_z
        off_x, off_y, off_z = [row_of_cells(offsets_ref, (d, i), k) for d in range(3)]
        gap_x, gap_z = point_gaps(off_x, 16, 0.0), point_gaps(off_z, 16, 0.0)
        gap_y = point_gaps(off_y, width, shift_y)
        weight_x, slope_x = spline(gap_x), spline_slope(gap_x)
        weight_z, slope_z = spline(gap_z), spline_slope(gap_z)
        both_y = jnp.concatenate([spline(gap_y), spline_slope(gap_y)], axis=1)
        y_high = both_y.astype(jnp.bfloat16)
        y_low = (both_y - y_high.astype(jnp.float32)).astype(jnp.bfloat16)
        parts = []
        for a in range(11):
            part = grid_ref[8 * i + a, pl.ds(pl.multiple_of(8 * k, 8), 16), :]
            low = part - part.astype(jnp.bfloat16).astype(jnp.float32)
            parts.append(jnp.where(middle, low, part).astype(jnp.bfloat16))
        found = jnp.dot(
            jnp.concatenate(parts, axis=0),
            jnp.concatenate([y_high, y_high, y_low], axis=0),
            preferred_element_type=jnp.float32,
        )
        lanes = cells_y * slots
        totals = [jnp.zeros((16, lanes), jnp.float32) for _ in range(3)]
        for a in range(11):
            level = found[16 * a : 16 * a + 16, :lanes]
            rising = found[16 * a : 16 * a + 16, lanes:]
            totals[0] += slope_x[a : a + 1] * level
            totals[1] += weight_x[a : a + 1] * rising
            totals[2] += weight_x[a : a + 1] * level
        charge = row_of_cells(weighted_ref, (i,), k)
        for d, along_z in enumerate((weight_z, weight_z, slope_z)):
            force = -charge * jnp.sum(totals[d] * along_z, axis=0, keepdims=True)
            for j in range(cells_y):
                out_ref[d, i, j, pl.ds(k, 1), :] = force[:, j * slots : (j + 1) * slots]
        return carry

    lax.fori_loop(0, cells_x * cells_z, body, 0)


def grid_forces(offsets, weighted, potential):
    cells_x, cells_y, cells_z, _ = weighted.shape
    width = 8 * cells_y + 16
    grid = jnp.transpose(potential[1:, 1:, 1:], (0, 2, 1))
    grid = jnp.pad(grid, ((0, 0), (0, 8 * cells_z + 8 - grid.shape[1]), (0, width - grid.shape[2])))
    grid = jnp.concatenate([grid] * 3, axis=2)
    return pl.pallas_call(
        gather_kernel,
        out_shape=jax.ShapeDtypeStruct(offsets.shape, jnp.float32),
        in_specs=[pl.BlockSpec(memory_space=pltpu.VMEM)] * 3,
        out_specs=pl.BlockSpec(memory_space=pltpu.VMEM),
        compiler_params=pltpu.CompilerParams(vmem_limit_bytes=24 * 2**20),
        cost_estimate=pl.CostEstimate(flops=10**8, bytes_accessed=4 * 10**6, transcendentals=0),
    )(offsets, weighted, grid)


def spread_halo(value, sides, depth):
    for axis, dim in sides:
        size, length = (lax.axis_size(axis), value.shape[dim] - 3)
        up = [(i, (i + 1) % size) for i in range(size - 1)]
        down = [(j, i) for i, j in up]
        last = lax.slice_in_dim(value, length - depth + 1, length + 3, axis=dim)
        initial = lax.slice_in_dim(value, 0, depth + 1, axis=dim)
        before = lax.ppermute(last, axis, up)
        after = lax.ppermute(initial, axis, down)

        def placed(part, low, high):
            widths = [(0, 0)] * part.ndim
            widths[dim] = (low, high)
            return jnp.pad(part, widths)

        value = (
            placed(value, depth - 1, depth - 2)
            + placed(before, 0, length + depth - 2)
            + placed(after, length + depth - 1, 0)
        )
    return value


def coarse_halo(value, sides, known, depth):
    for axis, dim in sides:
        size, length = (lax.axis_size(axis), value.shape[dim] - 2 * known - 1)
        up = [(i, (i + 1) % size) for i in range(size - 1)]
        down = [(j, i) for i, j in up]
        start = length - depth + known
        last = lax.slice_in_dim(value, start, start + depth - known, axis=dim)
        initial = lax.slice_in_dim(value, 2 * known + 1, depth + known, axis=dim)
        before = lax.ppermute(last, axis, up)
        after = lax.ppermute(initial, axis, down)
        value = jnp.concatenate([before, value, after], axis=dim)
    return value


def kernel_band(in_length, spread):
    row_index = jnp.arange(in_length)[:, None]
    column_index = jnp.arange(in_length - 16)[None, :]
    distance = row_index - column_index - 8
    gap = distance.astype(jnp.float32)
    return jnp.where(jnp.abs(distance) <= 8, jnp.exp(-gap * gap / (2.0 * spread * spread)), 0.0)


def along_axis(values, matrix, where_axis):
    contracted = jnp.tensordot(values, matrix, axes=([where_axis], [0]), precision=highest)
    return jnp.moveaxis(contracted, -1, where_axis)


def convolve(values, spread, strength):
    for where_axis in range(3):
        values = along_axis(values, kernel_band(values.shape[where_axis], spread), where_axis)
    return strength * values


def grid_map(fine_length, coarse_length, fine_start, coarse_start):
    fine_index = jnp.arange(fine_length)[:, None] + fine_start
    coarse_index = jnp.arange(coarse_length)[None, :] + coarse_start
    gap = fine_index - 2 * coarse_index
    return jnp.where(gap == 0, 1.0, jnp.where(jnp.abs(gap) == 1, 0.5, 0.0)).astype(jnp.float32)


def cell_positions(offsets, first_cell):
    coordinates = []
    for dimension in range(3):
        cell_count = offsets.shape[dimension + 1]
        cell_index = jnp.arange(cell_count).astype(jnp.float32) + first_cell
        broadcast_shape = [1, 1, 1, 1]
        broadcast_shape[dimension] = cell_count
        coordinates.append((cell_index.reshape(broadcast_shape) + offsets[dimension]))
    return jnp.stack(coordinates)


def short_kernel(counts_ref, grown_ref, partners_ref, out_ref, own_s, acc_s):
    _, cells_x, cells_y, cells_z, slots = out_ref.shape
    lane = lax.broadcasted_iota(jnp.int32, (1, slots), 1)

    def cell_body(cell, carry):
        i = cell // (cells_y * cells_z)
        j = (cell // cells_z) % cells_y
        k = cell % cells_z
        count = counts_ref[cell]
        own_rows = [grown_ref[d, i + 1, j + 1, pl.ds(k + 1, 1), :] for d in range(3)]
        for d in range(3):
            own_s[d] = jnp.broadcast_to(own_rows[d], (slots, slots)).T

        def block_body(block, carry):
            row = pl.multiple_of(block * 8, 8)
            own = [own_s[d, pl.ds(row, 8), :] for d in range(3)]
            total = [jnp.zeros((8, slots), jnp.float32) for _ in range(3)]
            for step_x in range(3):
                for step_y in range(3):
                    for step_z in range(3):
                        near = [
                            grown_ref[d, i + step_x, j + step_y, pl.ds(k + step_z, 1), :]
                            for d in range(4)
                        ]
                        gap = [own[d] - near[d] for d in range(3)]
                        distance_sq = gap[0] * gap[0] + gap[1] * gap[1] + gap[2] * gap[2]
                        reach = jnp.maximum(1.0 - distance_sq, 0.0)
                        below = 1.015625 - reach
                        inverse = pl.reciprocal(below, approx=True)
                        strength = (reach * reach) * (reach * near[3]) * inverse
                        total = [total[d] + strength * gap[d] for d in range(3)]
            for d in range(3):
                acc_s[d, pl.ds(row, 8), :] = total[d]
            return carry

        lax.fori_loop(0, (count + 7) // 8, block_body, 0)
        charge = grown_ref[3, i + 1, j + 1, pl.ds(k + 1, 1), :]
        partner = partners_ref[i, j, pl.ds(k, 1), :]
        bonded = (lane < count) & (partner < count)
        index = jnp.broadcast_to(partner, (8, slots))
        for d in range(3):
            pair = 0.125 * charge * jnp.sum(acc_s[d].T, axis=0, keepdims=True)
            source = jnp.broadcast_to(own_rows[d], (8, slots))
            other = jnp.take_along_axis(source, index, axis=1)[0:1]
            bond = jnp.where(bonded, (-8.0 * bond_spring) * (own_rows[d] - other), 0.0)
            out_ref[d, i, j, pl.ds(k, 1), :] = jnp.where(lane < count, pair, 0.0) + bond
        return carry

    lax.fori_loop(0, cells_x * cells_y * cells_z, cell_body, 0)


def short_forces(counts, grown, partners):
    cells, slots = counts.shape, partners.shape[-1]
    return pl.pallas_call(
        short_kernel,
        out_shape=jax.ShapeDtypeStruct((3,) + cells + (slots,), jnp.float32),
        in_specs=[pl.BlockSpec(memory_space=pltpu.SMEM)]
        + [pl.BlockSpec(memory_space=pltpu.VMEM)] * 2,
        out_specs=pl.BlockSpec(memory_space=pltpu.VMEM),
        scratch_shapes=[pltpu.VMEM((3, slots, slots), jnp.float32)] * 2,
        compiler_params=pltpu.CompilerParams(vmem_limit_bytes=24 * 2**20),
        cost_estimate=pl.CostEstimate(flops=10**9, bytes_accessed=10**7, transcendentals=10**7),
    )(counts.reshape(-1), grown, partners)


def inside_mask(lengths, depth):
    mask = jnp.float32(1.0)
    for dim, axis in enumerate(("gx", "gy", "ga")):
        length = lengths[dim]
        first = lax.axis_index(axis) * length - depth
        point = jnp.arange(length + 2 * depth) + first
        inside = (point >= 0) & (point < length * lax.axis_size(axis))
        shape = [1, 1, 1]
        shape[dim] = length + 2 * depth
        mask = mask * inside.astype(jnp.float32).reshape(shape)
    return mask


def per_device(offsets, charge, counts, partners):
    slot_count = charge.shape[-1]
    cells_x, cells_y, cells_z = charge.shape[:3]
    in_use = (jnp.arange(slot_count) < counts[..., None]).astype(jnp.float32)
    weighted = charge * in_use
    packed = jnp.concatenate([offsets, weighted[None]], axis=0)
    grown_tiles = padded_2(packed, (("gx", 1), ("gy", 2), ("ga", 3)), 1)
    grown_offsets = grown_tiles[:3]
    grown_charge = grown_tiles[3]
    cell_units = cell_positions(grown_offsets, -1.0)
    grown = jnp.concatenate([cell_units, grown_charge[None]], axis=0)
    short_force = short_forces(counts, grown, partners)
    grid_x, grid_y, grid_z = (8 * cells_x, 8 * cells_y, 8 * cells_z)
    lengths = (grid_x, grid_y, grid_z)
    halo_depth = 10
    spread = spread_charge(offsets, weighted)
    widened = spread_halo(spread, (("ga", 2), ("gx", 0), ("gy", 1)), halo_depth)
    widened = widened * inside_mask(lengths, halo_depth)
    fine_potential = convolve(widened, fine_spread, fine_scale)
    known, coarse_depth = ((halo_depth - 1) // 2, 10)
    coarse_lengths = tuple(length // 2 for length in lengths)
    coarse_charge = widened
    for where_axis, fine_length in enumerate(lengths):
        coarse_charge = along_axis(
            coarse_charge,
            grid_map(
                fine_length + 2 * halo_depth,
                fine_length // 2 + 2 * known + 1,
                -halo_depth,
                -known,
            ),
            where_axis,
        )
    grown_coarse = coarse_halo(coarse_charge, (("ga", 2), ("gx", 0), ("gy", 1)), known, coarse_depth)
    grown_coarse = grown_coarse * inside_mask(coarse_lengths, coarse_depth)
    potential = convolve(grown_coarse, coarse_spread, coarse_scale)
    potential = potential * inside_mask(coarse_lengths, 2)
    for where_axis, fine_length in enumerate(lengths):
        potential = along_axis(
            potential,
            jnp.transpose(grid_map(fine_length + 4, fine_length // 2 + 4, -2, -2)),
            where_axis,
        )
    potential = (potential + fine_potential) * inside_mask(lengths, 2)
    long_force = grid_forces(offsets, weighted, potential)
    return (short_force, long_force)


def solution(mesh):
    return jax.shard_map(
        per_device,
        mesh=mesh,
        in_specs=(
            P(None, "gx", "gy", "ga", None),
            P("gx", "gy", "ga", None),
            P("gx", "gy", "ga"),
            P("gx", "gy", "ga", None),
        ),
        out_specs=(P(None, "gx", "gy", "ga", None), P(None, "gx", "gy", "ga", None)),
        check_vma=False,
    )
```

```python
import jax
import jax.numpy as jnp
from jax import lax
from jax.experimental import pallas as pl
from jax.experimental.pallas import tpu as pltpu
from jax.sharding import PartitionSpec as P

highest = lax.Precision.HIGHEST
bond_spring = 0.1
fine_scale = 4.0
coarse_scale = 2.0
fine_spread = 2.5
coarse_spread = 6.0


def padded_2(value, sides, width):
    for axis, dim in sides:
        size, length = (lax.axis_size(axis), value.shape[dim])
        up = [(i, (i + 1) % size) for i in range(size - 1)]
        down = [(j, i) for i, j in up]
        last = lax.slice_in_dim(value, length - width, length, axis=dim)
        initial = lax.slice_in_dim(value, 0, width, axis=dim)
        before = lax.ppermute(last, axis, up)
        after = lax.ppermute(initial, axis, down)
        value = jnp.concatenate([before, value, after], axis=dim)
    return value


def spline(shifted):
    magnitude = jnp.abs(shifted)
    margin = jnp.maximum(1.5 - magnitude, 0.0)
    return jnp.where(magnitude < 0.5, 0.75 - shifted * shifted, 0.5 * margin * margin)


def spline_slope(shifted):
    magnitude = jnp.abs(shifted)
    margin = jnp.maximum(1.5 - magnitude, 0.0)
    return jnp.where(magnitude < 0.5, -2.0 * shifted, jnp.where(shifted > 0.0, -margin, margin))


def split_product(left, right, dims):
    left_high, right_high = left.astype(jnp.bfloat16), right.astype(jnp.bfloat16)
    left_low = (left - left_high.astype(jnp.float32)).astype(jnp.bfloat16)
    right_low = (right - right_high.astype(jnp.float32)).astype(jnp.bfloat16)

    def product(one, other):
        return lax.dot_general(one, other, (dims, ((), ())), preferred_element_type=jnp.float32)

    return product(left_high, right_high) + (
        product(left_low, right_high) + product(left_high, right_low)
    )


def row_of_cells(ref, lead, k):
    return jnp.concatenate([ref[lead + (j, pl.ds(k, 1))] for j in range(ref.shape[-3])], axis=1)


def point_gaps(offset, count, shift):
    points = lax.broadcasted_iota(jnp.int32, (count, offset.shape[1]), 0).astype(jnp.float32)
    return (8.0 * offset + 1.0 + shift) - points


def cell_shift(cells_y, slots):
    lane = lax.broadcasted_iota(jnp.int32, (1, cells_y * slots), 1)
    return 8.0 * (lane // slots).astype(jnp.float32)


def spread_kernel(offsets_ref, weighted_ref, grid_ref):
    cells_x, cells_y, cells_z, slots = weighted_ref.shape
    width = grid_ref.shape[-1]
    grid_ref[...] = jnp.zeros_like(grid_ref)
    shift_y = cell_shift(cells_y, slots)

    def body(step, carry):
        i, k = step // cells_z, step % cells_z
        off_x, off_y, off_z = [row_of_cells(offsets_ref, (d, i), k) for d in range(3)]
        charge = row_of_cells(weighted_ref, (i,), k)
        weight_x = spline(point_gaps(off_x, 16, 0.0)) * charge
        weight_z = spline(point_gaps(off_z, 16, 0.0))
        weight_y = spline(point_gaps(off_y, width, shift_y))
        plane = jnp.concatenate([weight_x[a : a + 1] * weight_z for a in range(11)], axis=0)
        patch = split_product(plane, weight_y, ((1,), (1,)))
        for a in range(11):
            rows = pl.ds(pl.multiple_of(8 * k, 8), 16)
            grid_ref[8 * i + a, rows, :] += patch[16 * a : 16 * a + 16]
        return carry

    lax.fori_loop(0, cells_x * cells_z, body, 0)


def spread_charge(offsets, weighted):
    cells_x, cells_y, cells_z, _ = weighted.shape
    width = 8 * cells_y + 16
    grid = pl.pallas_call(
        spread_kernel,
        out_shape=jax.ShapeDtypeStruct((8 * cells_x + 3, 8 * cells_z + 8, width), jnp.float32),
        in_specs=[pl.BlockSpec(memory_space=pltpu.VMEM)] * 2,
        out_specs=pl.BlockSpec(memory_space=pltpu.VMEM),
        compiler_params=pltpu.CompilerParams(vmem_limit_bytes=24 * 2**20),
        cost_estimate=pl.CostEstimate(flops=10**8, bytes_accessed=4 * 10**6, transcendentals=0),
    )(offsets, weighted)
    return jnp.transpose(grid[:, : 8 * cells_z + 3, : 8 * cells_y + 3], (0, 2, 1))


def gather_kernel(offsets_ref, weighted_ref, grid_ref, out_ref):
    cells_x, cells_y, cells_z, slots = weighted_ref.shape
    width = grid_ref.shape[-1] // 3
    shift_y = cell_shift(cells_y, slots)
    lane = lax.broadcasted_iota(jnp.int32, (16, 3 * width), 1)
    middle = (lane >= width) & (lane < 2 * width)

    def body(step, carry):
        i, k = step // cells_z, step % cells_z
        off_x, off_y, off_z = [row_of_cells(offsets_ref, (d, i), k) for d in range(3)]
        gap_x, gap_z = point_gaps(off_x, 16, 0.0), point_gaps(off_z, 16, 0.0)
        gap_y = point_gaps(off_y, width, shift_y)
        weight_x, slope_x = spline(gap_x), spline_slope(gap_x)
        weight_z, slope_z = spline(gap_z), spline_slope(gap_z)
        both_y = jnp.concatenate([spline(gap_y), spline_slope(gap_y)], axis=1)
        y_high = both_y.astype(jnp.bfloat16)
        y_low = (both_y - y_high.astype(jnp.float32)).astype(jnp.bfloat16)
        parts = []
        for a in range(11):
            part = grid_ref[8 * i + a, pl.ds(pl.multiple_of(8 * k, 8), 16), :]
            low = part - part.astype(jnp.bfloat16).astype(jnp.float32)
            parts.append(jnp.where(middle, low, part).astype(jnp.bfloat16))
        found = jnp.dot(
            jnp.concatenate(parts, axis=0),
            jnp.concatenate([y_high, y_high, y_low], axis=0),
            preferred_element_type=jnp.float32,
        )
        lanes = cells_y * slots
        totals = [jnp.zeros((16, lanes), jnp.float32) for _ in range(3)]
        for a in range(11):
            level = found[16 * a : 16 * a + 16, :lanes]
            rising = found[16 * a : 16 * a + 16, lanes:]
            totals[0] += slope_x[a : a + 1] * level
            totals[1] += weight_x[a : a + 1] * rising
            totals[2] += weight_x[a : a + 1] * level
        charge = row_of_cells(weighted_ref, (i,), k)
        for d, along_z in enumerate((weight_z, weight_z, slope_z)):
            force = -charge * jnp.sum(totals[d] * along_z, axis=0, keepdims=True)
            for j in range(cells_y):
                out_ref[d, i, j, pl.ds(k, 1), :] = force[:, j * slots : (j + 1) * slots]
        return carry

    lax.fori_loop(0, cells_x * cells_z, body, 0)


def grid_forces(offsets, weighted, potential):
    cells_x, cells_y, cells_z, _ = weighted.shape
    width = 8 * cells_y + 16
    grid = jnp.transpose(potential[1:, 1:, 1:], (0, 2, 1))
    grid = jnp.pad(grid, ((0, 0), (0, 8 * cells_z + 8 - grid.shape[1]), (0, width - grid.shape[2])))
    grid = jnp.concatenate([grid] * 3, axis=2)
    return pl.pallas_call(
        gather_kernel,
        out_shape=jax.ShapeDtypeStruct(offsets.shape, jnp.float32),
        in_specs=[pl.BlockSpec(memory_space=pltpu.VMEM)] * 3,
        out_specs=pl.BlockSpec(memory_space=pltpu.VMEM),
        compiler_params=pltpu.CompilerParams(vmem_limit_bytes=24 * 2**20),
        cost_estimate=pl.CostEstimate(flops=10**8, bytes_accessed=4 * 10**6, transcendentals=0),
    )(offsets, weighted, grid)


def spread_halo(value, sides, depth):
    for axis, dim in sides:
        size, length = (lax.axis_size(axis), value.shape[dim] - 3)
        up = [(i, (i + 1) % size) for i in range(size - 1)]
        down = [(j, i) for i, j in up]
        last = lax.slice_in_dim(value, length - depth + 1, length + 3, axis=dim)
        initial = lax.slice_in_dim(value, 0, depth + 1, axis=dim)
        before = lax.ppermute(last, axis, up)
        after = lax.ppermute(initial, axis, down)

        def placed(part, low, high):
            widths = [(0, 0)] * part.ndim
            widths[dim] = (low, high)
            return jnp.pad(part, widths)

        value = (
            placed(value, depth - 1, depth - 2)
            + placed(before, 0, length + depth - 2)
            + placed(after, length + depth - 1, 0)
        )
    return value


def coarse_halo(value, sides, known, depth):
    for axis, dim in sides:
        size, length = (lax.axis_size(axis), value.shape[dim] - 2 * known - 1)
        up = [(i, (i + 1) % size) for i in range(size - 1)]
        down = [(j, i) for i, j in up]
        start = length - depth + known
        last = lax.slice_in_dim(value, start, start + depth - known, axis=dim)
        initial = lax.slice_in_dim(value, 2 * known + 1, depth + known, axis=dim)
        before = lax.ppermute(last, axis, up)
        after = lax.ppermute(initial, axis, down)
        value = jnp.concatenate([before, value, after], axis=dim)
    return value


def kernel_band(in_length, spread):
    row_index = jnp.arange(in_length)[:, None]
    column_index = jnp.arange(in_length - 16)[None, :]
    distance = row_index - column_index - 8
    gap = distance.astype(jnp.float32)
    return jnp.where(jnp.abs(distance) <= 8, jnp.exp(-gap * gap / (2.0 * spread * spread)), 0.0)


def along_axis(values, matrix, where_axis):
    contracted = jnp.tensordot(values, matrix, axes=([where_axis], [0]), precision=highest)
    return jnp.moveaxis(contracted, -1, where_axis)


def convolve(values, spread, strength):
    for where_axis in range(3):
        values = along_axis(values, kernel_band(values.shape[where_axis], spread), where_axis)
    return strength * values


def grid_map(fine_length, coarse_length, fine_start, coarse_start):
    fine_index = jnp.arange(fine_length)[:, None] + fine_start
    coarse_index = jnp.arange(coarse_length)[None, :] + coarse_start
    gap = fine_index - 2 * coarse_index
    return jnp.where(gap == 0, 1.0, jnp.where(jnp.abs(gap) == 1, 0.5, 0.0)).astype(jnp.float32)


def cell_positions(offsets, first_cell):
    coordinates = []
    for dimension in range(3):
        cell_count = offsets.shape[dimension + 1]
        cell_index = jnp.arange(cell_count).astype(jnp.float32) + first_cell
        broadcast_shape = [1, 1, 1, 1]
        broadcast_shape[dimension] = cell_count
        coordinates.append((cell_index.reshape(broadcast_shape) + offsets[dimension]))
    return jnp.stack(coordinates)


def short_kernel(counts_ref, grown_ref, partners_ref, out_ref, own_s, acc_s, near_s):
    _, cells_x, cells_y, cells_z, slots = out_ref.shape
    lane = lax.broadcasted_iota(jnp.int32, (1, slots), 1)

    def fill_body(column, carry):
        i, j = column // (cells_y + 2), column % (cells_y + 2)
        for k in range(cells_z + 2):
            for d in range(4):
                near_s[i, j, k, d] = jnp.broadcast_to(grown_ref[d, i, j, k : k + 1, :], (8, slots))
        return carry

    lax.fori_loop(0, (cells_x + 2) * (cells_y + 2), fill_body, 0)

    def cell_body(cell, carry):
        i = cell // (cells_y * cells_z)
        j = (cell // cells_z) % cells_y
        k = cell % cells_z
        count = counts_ref[cell]
        own_rows = [grown_ref[d, i + 1, j + 1, pl.ds(k + 1, 1), :] for d in range(3)]
        for d in range(3):
            own_s[d] = jnp.broadcast_to(own_rows[d], (slots, slots)).T

        def block_body(block, carry):
            row = pl.multiple_of(block * 8, 8)
            own = [own_s[d, pl.ds(row, 8), :] for d in range(3)]
            total = [jnp.zeros((8, slots), jnp.float32) for _ in range(3)]
            for step_x in range(3):
                for step_y in range(3):
                    for step_z in range(3):
                        near = [
                            near_s[i + step_x, j + step_y, k + step_z, d]
                            for d in range(4)
                        ]
                        gap = [own[d] - near[d] for d in range(3)]
                        distance_sq = gap[0] * gap[0] + gap[1] * gap[1] + gap[2] * gap[2]
                        reach = jnp.maximum(1.0 - distance_sq, 0.0)
                        below = 1.015625 - reach
                        inverse = pl.reciprocal(below, approx=True)
                        strength = (reach * reach) * (reach * near[3]) * inverse
                        total = [total[d] + strength * gap[d] for d in range(3)]
            for d in range(3):
                acc_s[d, pl.ds(row, 8), :] = total[d]
            return carry

        lax.fori_loop(0, (count + 7) // 8, block_body, 0)
        charge = grown_ref[3, i + 1, j + 1, pl.ds(k + 1, 1), :]
        partner = partners_ref[i, j, pl.ds(k, 1), :]
        bonded = (lane < count) & (partner < count)
        index = jnp.broadcast_to(partner, (8, slots))
        for d in range(3):
            pair = 0.125 * charge * jnp.sum(acc_s[d].T, axis=0, keepdims=True)
            source = jnp.broadcast_to(own_rows[d], (8, slots))
            other = jnp.take_along_axis(source, index, axis=1)[0:1]
            bond = jnp.where(bonded, (-8.0 * bond_spring) * (own_rows[d] - other), 0.0)
            out_ref[d, i, j, pl.ds(k, 1), :] = jnp.where(lane < count, pair, 0.0) + bond
        return carry

    lax.fori_loop(0, cells_x * cells_y * cells_z, cell_body, 0)


def short_forces(counts, grown, partners):
    cells, slots = counts.shape, partners.shape[-1]
    return pl.pallas_call(
        short_kernel,
        out_shape=jax.ShapeDtypeStruct((3,) + cells + (slots,), jnp.float32),
        in_specs=[pl.BlockSpec(memory_space=pltpu.SMEM)]
        + [pl.BlockSpec(memory_space=pltpu.VMEM)] * 2,
        out_specs=pl.BlockSpec(memory_space=pltpu.VMEM),
        scratch_shapes=[pltpu.VMEM((3, slots, slots), jnp.float32)] * 2
        + [pltpu.VMEM(grown.shape[1:4] + (4, 8, slots), jnp.float32)],
        compiler_params=pltpu.CompilerParams(vmem_limit_bytes=24 * 2**20),
        cost_estimate=pl.CostEstimate(flops=10**9, bytes_accessed=10**7, transcendentals=10**7),
    )(counts.reshape(-1), grown, partners)


def inside_mask(lengths, depth):
    mask = jnp.float32(1.0)
    for dim, axis in enumerate(("gx", "gy", "ga")):
        length = lengths[dim]
        first = lax.axis_index(axis) * length - depth
        point = jnp.arange(length + 2 * depth) + first
        inside = (point >= 0) & (point < length * lax.axis_size(axis))
        shape = [1, 1, 1]
        shape[dim] = length + 2 * depth
        mask = mask * inside.astype(jnp.float32).reshape(shape)
    return mask


def per_device(offsets, charge, counts, partners):
    slot_count = charge.shape[-1]
    cells_x, cells_y, cells_z = charge.shape[:3]
    in_use = (jnp.arange(slot_count) < counts[..., None]).astype(jnp.float32)
    weighted = charge * in_use
    packed = jnp.concatenate([offsets, weighted[None]], axis=0)
    grown_tiles = padded_2(packed, (("gx", 1), ("gy", 2), ("ga", 3)), 1)
    grown_offsets = grown_tiles[:3]
    grown_charge = grown_tiles[3]
    cell_units = cell_positions(grown_offsets, -1.0)
    grown = jnp.concatenate([cell_units, grown_charge[None]], axis=0)
    short_force = short_forces(counts, grown, partners)
    grid_x, grid_y, grid_z = (8 * cells_x, 8 * cells_y, 8 * cells_z)
    lengths = (grid_x, grid_y, grid_z)
    halo_depth = 10
    spread = spread_charge(offsets, weighted)
    widened = spread_halo(spread, (("ga", 2), ("gx", 0), ("gy", 1)), halo_depth)
    widened = widened * inside_mask(lengths, halo_depth)
    fine_potential = convolve(widened, fine_spread, fine_scale)
    known, coarse_depth = ((halo_depth - 1) // 2, 10)
    coarse_lengths = tuple(length // 2 for length in lengths)
    coarse_charge = widened
    for where_axis, fine_length in enumerate(lengths):
        coarse_charge = along_axis(
            coarse_charge,
            grid_map(
                fine_length + 2 * halo_depth,
                fine_length // 2 + 2 * known + 1,
                -halo_depth,
                -known,
            ),
            where_axis,
        )
    grown_coarse = coarse_halo(coarse_charge, (("ga", 2), ("gx", 0), ("gy", 1)), known, coarse_depth)
    grown_coarse = grown_coarse * inside_mask(coarse_lengths, coarse_depth)
    potential = convolve(grown_coarse, coarse_spread, coarse_scale)
    potential = potential * inside_mask(coarse_lengths, 2)
    for where_axis, fine_length in enumerate(lengths):
        potential = along_axis(
            potential,
            jnp.transpose(grid_map(fine_length + 4, fine_length // 2 + 4, -2, -2)),
            where_axis,
        )
    potential = (potential + fine_potential) * inside_mask(lengths, 2)
    long_force = grid_forces(offsets, weighted, potential)
    return (short_force, long_force)


def solution(mesh):
    return jax.shard_map(
        per_device,
        mesh=mesh,
        in_specs=(
            P(None, "gx", "gy", "ga", None),
            P("gx", "gy", "ga", None),
            P("gx", "gy", "ga"),
            P("gx", "gy", "ga", None),
        ),
        out_specs=(P(None, "gx", "gy", "ga", None), P(None, "gx", "gy", "ga", None)),
        check_vma=False,
    )
```

```python
import jax
import jax.numpy as jnp
from jax import lax
from jax.experimental import pallas as pl
from jax.experimental.pallas import tpu as pltpu
from jax.sharding import PartitionSpec as P

highest = lax.Precision.HIGHEST
bond_spring = 0.1
fine_scale = 4.0
coarse_scale = 2.0
fine_spread = 2.5
coarse_spread = 6.0


def padded_2(value, sides, width):
    for axis, dim in sides:
        size, length = (lax.axis_size(axis), value.shape[dim])
        up = [(i, (i + 1) % size) for i in range(size - 1)]
        down = [(j, i) for i, j in up]
        last = lax.slice_in_dim(value, length - width, length, axis=dim)
        initial = lax.slice_in_dim(value, 0, width, axis=dim)
        before = lax.ppermute(last, axis, up)
        after = lax.ppermute(initial, axis, down)
        value = jnp.concatenate([before, value, after], axis=dim)
    return value


def spline(shifted):
    magnitude = jnp.abs(shifted)
    margin = jnp.maximum(1.5 - magnitude, 0.0)
    return jnp.where(magnitude < 0.5, 0.75 - shifted * shifted, 0.5 * margin * margin)


def spline_slope(shifted):
    magnitude = jnp.abs(shifted)
    margin = jnp.maximum(1.5 - magnitude, 0.0)
    return jnp.where(magnitude < 0.5, -2.0 * shifted, jnp.where(shifted > 0.0, -margin, margin))


def split_product(left, right, dims):
    left_high, right_high = left.astype(jnp.bfloat16), right.astype(jnp.bfloat16)
    left_low = (left - left_high.astype(jnp.float32)).astype(jnp.bfloat16)
    right_low = (right - right_high.astype(jnp.float32)).astype(jnp.bfloat16)

    def product(one, other):
        return lax.dot_general(one, other, (dims, ((), ())), preferred_element_type=jnp.float32)

    return product(left_high, right_high) + (
        product(left_low, right_high) + product(left_high, right_low)
    )


def row_of_cells(ref, lead, k):
    return jnp.concatenate([ref[lead + (j, pl.ds(k, 1))] for j in range(ref.shape[-3])], axis=1)


def point_gaps(offset, count, shift):
    points = lax.broadcasted_iota(jnp.int32, (count, offset.shape[1]), 0).astype(jnp.float32)
    return (8.0 * offset + 1.0 + shift) - points


def cell_shift(cells_y, slots):
    lane = lax.broadcasted_iota(jnp.int32, (1, cells_y * slots), 1)
    return 8.0 * (lane // slots).astype(jnp.float32)


def spread_kernel(offsets_ref, weighted_ref, grid_ref):
    cells_x, cells_y, cells_z, slots = weighted_ref.shape
    width = grid_ref.shape[-1]
    grid_ref[...] = jnp.zeros_like(grid_ref)
    shift_y = cell_shift(cells_y, slots)

    def body(step, carry):
        i, k = step // cells_z, step % cells_z
        off_x, off_y, off_z = [row_of_cells(offsets_ref, (d, i), k) for d in range(3)]
        charge = row_of_cells(weighted_ref, (i,), k)
        weight_x = spline(point_gaps(off_x, 16, 0.0)) * charge
        weight_z = spline(point_gaps(off_z, 16, 0.0))
        weight_y = spline(point_gaps(off_y, width, shift_y))
        plane = jnp.concatenate([weight_x[a : a + 1] * weight_z for a in range(11)], axis=0)
        patch = split_product(plane, weight_y, ((1,), (1,)))
        for a in range(11):
            rows = pl.ds(pl.multiple_of(8 * k, 8), 16)
            grid_ref[8 * i + a, rows, :] += patch[16 * a : 16 * a + 16]
        return carry

    lax.fori_loop(0, cells_x * cells_z, body, 0)


def spread_charge(offsets, weighted):
    cells_x, cells_y, cells_z, _ = weighted.shape
    width = 8 * cells_y + 16
    grid = pl.pallas_call(
        spread_kernel,
        out_shape=jax.ShapeDtypeStruct((8 * cells_x + 3, 8 * cells_z + 8, width), jnp.float32),
        in_specs=[pl.BlockSpec(memory_space=pltpu.VMEM)] * 2,
        out_specs=pl.BlockSpec(memory_space=pltpu.VMEM),
        compiler_params=pltpu.CompilerParams(vmem_limit_bytes=24 * 2**20),
        cost_estimate=pl.CostEstimate(flops=10**8, bytes_accessed=4 * 10**6, transcendentals=0),
    )(offsets, weighted)
    return jnp.transpose(grid[:, : 8 * cells_z + 3, : 8 * cells_y + 3], (0, 2, 1))


def gather_kernel(offsets_ref, weighted_ref, grid_ref, out_ref):
    cells_x, cells_y, cells_z, slots = weighted_ref.shape
    width = grid_ref.shape[-1] // 3
    shift_y = cell_shift(cells_y, slots)
    lane = lax.broadcasted_iota(jnp.int32, (16, 3 * width), 1)
    middle = (lane >= width) & (lane < 2 * width)

    def body(step, carry):
        i, k = step // cells_z, step % cells_z
        off_x, off_y, off_z = [row_of_cells(offsets_ref, (d, i), k) for d in range(3)]
        gap_x, gap_z = point_gaps(off_x, 16, 0.0), point_gaps(off_z, 16, 0.0)
        gap_y = point_gaps(off_y, width, shift_y)
        weight_x, slope_x = spline(gap_x), spline_slope(gap_x)
        weight_z, slope_z = spline(gap_z), spline_slope(gap_z)
        both_y = jnp.concatenate([spline(gap_y), spline_slope(gap_y)], axis=1)
        y_high = both_y.astype(jnp.bfloat16)
        y_low = (both_y - y_high.astype(jnp.float32)).astype(jnp.bfloat16)
        parts = []
        for a in range(11):
            part = grid_ref[8 * i + a, pl.ds(pl.multiple_of(8 * k, 8), 16), :]
            low = part - part.astype(jnp.bfloat16).astype(jnp.float32)
            parts.append(jnp.where(middle, low, part).astype(jnp.bfloat16))
        found = jnp.dot(
            jnp.concatenate(parts, axis=0),
            jnp.concatenate([y_high, y_high, y_low], axis=0),
            preferred_element_type=jnp.float32,
        )
        lanes = cells_y * slots
        totals = [jnp.zeros((16, lanes), jnp.float32) for _ in range(3)]
        for a in range(11):
            level = found[16 * a : 16 * a + 16, :lanes]
            rising = found[16 * a : 16 * a + 16, lanes:]
            totals[0] += slope_x[a : a + 1] * level
            totals[1] += weight_x[a : a + 1] * rising
            totals[2] += weight_x[a : a + 1] * level
        charge = row_of_cells(weighted_ref, (i,), k)
        for d, along_z in enumerate((weight_z, weight_z, slope_z)):
            force = -charge * jnp.sum(totals[d] * along_z, axis=0, keepdims=True)
            for j in range(cells_y):
                out_ref[d, i, j, pl.ds(k, 1), :] = force[:, j * slots : (j + 1) * slots]
        return carry

    lax.fori_loop(0, cells_x * cells_z, body, 0)


def grid_forces(offsets, weighted, potential):
    cells_x, cells_y, cells_z, _ = weighted.shape
    width = 8 * cells_y + 16
    grid = jnp.transpose(potential[1:, 1:, 1:], (0, 2, 1))
    grid = jnp.pad(grid, ((0, 0), (0, 8 * cells_z + 8 - grid.shape[1]), (0, width - grid.shape[2])))
    grid = jnp.concatenate([grid] * 3, axis=2)
    return pl.pallas_call(
        gather_kernel,
        out_shape=jax.ShapeDtypeStruct(offsets.shape, jnp.float32),
        in_specs=[pl.BlockSpec(memory_space=pltpu.VMEM)] * 3,
        out_specs=pl.BlockSpec(memory_space=pltpu.VMEM),
        compiler_params=pltpu.CompilerParams(vmem_limit_bytes=24 * 2**20),
        cost_estimate=pl.CostEstimate(flops=10**8, bytes_accessed=4 * 10**6, transcendentals=0),
    )(offsets, weighted, grid)


def spread_halo(value, sides, depth):
    for axis, dim in sides:
        size, length = (lax.axis_size(axis), value.shape[dim] - 3)
        up = [(i, (i + 1) % size) for i in range(size - 1)]
        down = [(j, i) for i, j in up]
        last = lax.slice_in_dim(value, length - depth + 1, length + 3, axis=dim)
        initial = lax.slice_in_dim(value, 0, depth + 1, axis=dim)
        before = lax.ppermute(last, axis, up)
        after = lax.ppermute(initial, axis, down)

        def placed(part, low, high):
            widths = [(0, 0)] * part.ndim
            widths[dim] = (low, high)
            return jnp.pad(part, widths)

        value = (
            placed(value, depth - 1, depth - 2)
            + placed(before, 0, length + depth - 2)
            + placed(after, length + depth - 1, 0)
        )
    return value


def coarse_halo(value, sides, known, depth):
    for axis, dim in sides:
        size, length = (lax.axis_size(axis), value.shape[dim] - 2 * known - 1)
        up = [(i, (i + 1) % size) for i in range(size - 1)]
        down = [(j, i) for i, j in up]
        start = length - depth + known
        last = lax.slice_in_dim(value, start, start + depth - known, axis=dim)
        initial = lax.slice_in_dim(value, 2 * known + 1, depth + known, axis=dim)
        before = lax.ppermute(last, axis, up)
        after = lax.ppermute(initial, axis, down)
        value = jnp.concatenate([before, value, after], axis=dim)
    return value


def kernel_band(in_length, spread):
    row_index = jnp.arange(in_length)[:, None]
    column_index = jnp.arange(in_length - 16)[None, :]
    distance = row_index - column_index - 8
    gap = distance.astype(jnp.float32)
    return jnp.where(jnp.abs(distance) <= 8, jnp.exp(-gap * gap / (2.0 * spread * spread)), 0.0)


def along_axis(values, matrix, where_axis):
    contracted = jnp.tensordot(values, matrix, axes=([where_axis], [0]), precision=highest)
    return jnp.moveaxis(contracted, -1, where_axis)


def convolve(values, spread, strength):
    for where_axis in range(3):
        values = along_axis(values, kernel_band(values.shape[where_axis], spread), where_axis)
    return strength * values


def grid_map(fine_length, coarse_length, fine_start, coarse_start):
    fine_index = jnp.arange(fine_length)[:, None] + fine_start
    coarse_index = jnp.arange(coarse_length)[None, :] + coarse_start
    gap = fine_index - 2 * coarse_index
    return jnp.where(gap == 0, 1.0, jnp.where(jnp.abs(gap) == 1, 0.5, 0.0)).astype(jnp.float32)


def cell_positions(offsets, first_cell):
    coordinates = []
    for dimension in range(3):
        cell_count = offsets.shape[dimension + 1]
        cell_index = jnp.arange(cell_count).astype(jnp.float32) + first_cell
        broadcast_shape = [1, 1, 1, 1]
        broadcast_shape[dimension] = cell_count
        coordinates.append((cell_index.reshape(broadcast_shape) + offsets[dimension]))
    return jnp.stack(coordinates)


def short_kernel(counts_ref, grown_ref, partners_ref, out_ref, own_s, acc_s, near_s):
    _, cells_x, cells_y, cells_z, slots = out_ref.shape
    lane = lax.broadcasted_iota(jnp.int32, (1, slots), 1)

    part_row = lax.broadcasted_iota(jnp.int32, (16, slots), 0)
    pick_row = lax.broadcasted_iota(jnp.int32, (16, 3 * slots), 0)
    pick_lane = lax.broadcasted_iota(jnp.int32, (16, 3 * slots), 1)
    picked = (pick_row < 9) & (pick_row % 3 == pick_lane // slots)
    picker = jnp.where(picked, 1.0, 0.0).astype(jnp.bfloat16)
    ones = jnp.ones((16, slots), jnp.bfloat16)

    def fill_body(column, carry):
        i, j = column // (cells_y + 2), column % (cells_y + 2)
        for k in range(cells_z + 2):
            for d in range(4):
                near_s[i, j, k, d] = jnp.broadcast_to(grown_ref[d, i, j, k : k + 1, :], (8, slots))
        return carry

    lax.fori_loop(0, (cells_x + 2) * (cells_y + 2), fill_body, 0)

    def cell_body(cell, carry):
        i = cell // (cells_y * cells_z)
        j = (cell // cells_z) % cells_y
        k = cell % cells_z
        count = counts_ref[cell]
        own_rows = [grown_ref[d, i + 1, j + 1, pl.ds(k + 1, 1), :] for d in range(3)]
        rest = jnp.concatenate(own_rows * 3 + [jnp.zeros((7, slots), jnp.float32)], axis=0)
        high = rest.astype(jnp.bfloat16).astype(jnp.float32)
        middle = (rest - high).astype(jnp.bfloat16).astype(jnp.float32)
        low = rest - high - middle
        parts = jnp.where(part_row < 3, high, jnp.where(part_row < 6, middle, low))
        columns = lax.dot_general(
            parts.astype(jnp.bfloat16),
            picker,
            (((0,), (0,)), ((), ())),
            preferred_element_type=jnp.float32,
        )
        for d in range(3):
            own_s[d] = columns[:, d * slots : (d + 1) * slots]

        def block_body(block, carry):
            row = pl.multiple_of(block * 8, 8)
            own = [own_s[d, pl.ds(row, 8), :] for d in range(3)]
            total = [jnp.zeros((8, slots), jnp.float32) for _ in range(3)]
            for step_x in range(3):
                for step_y in range(3):
                    for step_z in range(3):
                        near = [
                            near_s[i + step_x, j + step_y, k + step_z, d]
                            for d in range(4)
                        ]
                        gap = [own[d] - near[d] for d in range(3)]
                        distance_sq = gap[0] * gap[0] + gap[1] * gap[1] + gap[2] * gap[2]
                        reach = jnp.maximum(1.0 - distance_sq, 0.0)
                        below = 1.015625 - reach
                        inverse = pl.reciprocal(below, approx=True)
                        strength = (reach * reach) * (reach * near[3]) * inverse
                        total = [total[d] + strength * gap[d] for d in range(3)]
            for d in range(3):
                acc_s[d, pl.ds(row, 8), :] = total[d]
            return carry

        lax.fori_loop(0, (count + 7) // 8, block_body, 0)
        charge = grown_ref[3, i + 1, j + 1, pl.ds(k + 1, 1), :]
        partner = partners_ref[i, j, pl.ds(k, 1), :]
        bonded = (lane < count) & (partner < count)
        index = jnp.broadcast_to(partner, (8, slots))
        sums = acc_s[...].reshape(3 * slots, slots)
        sums_high = sums.astype(jnp.bfloat16)
        sums_low = (sums - sums_high.astype(jnp.float32)).astype(jnp.bfloat16)
        sums_row = sum(
            lax.dot_general(
                ones, part, (((1,), (1,)), ((), ())), preferred_element_type=jnp.float32
            )
            for part in (sums_high, sums_low)
        )
        for d in range(3):
            pair = 0.125 * charge * sums_row[0:1, d * slots : (d + 1) * slots]
            source = jnp.broadcast_to(own_rows[d], (8, slots))
            other = jnp.take_along_axis(source, index, axis=1)[0:1]
            bond = jnp.where(bonded, (-8.0 * bond_spring) * (own_rows[d] - other), 0.0)
            out_ref[d, i, j, pl.ds(k, 1), :] = jnp.where(lane < count, pair, 0.0) + bond
        return carry

    lax.fori_loop(0, cells_x * cells_y * cells_z, cell_body, 0)


def short_forces(counts, grown, partners):
    cells, slots = counts.shape, partners.shape[-1]
    return pl.pallas_call(
        short_kernel,
        out_shape=jax.ShapeDtypeStruct((3,) + cells + (slots,), jnp.float32),
        in_specs=[pl.BlockSpec(memory_space=pltpu.SMEM)]
        + [pl.BlockSpec(memory_space=pltpu.VMEM)] * 2,
        out_specs=pl.BlockSpec(memory_space=pltpu.VMEM),
        scratch_shapes=[pltpu.VMEM((3, slots, slots), jnp.float32)] * 2
        + [pltpu.VMEM(grown.shape[1:4] + (4, 8, slots), jnp.float32)],
        compiler_params=pltpu.CompilerParams(vmem_limit_bytes=24 * 2**20),
        cost_estimate=pl.CostEstimate(flops=10**9, bytes_accessed=10**7, transcendentals=10**7),
    )(counts.reshape(-1), grown, partners)


def inside_mask(lengths, depth):
    mask = jnp.float32(1.0)
    for dim, axis in enumerate(("gx", "gy", "ga")):
        length = lengths[dim]
        first = lax.axis_index(axis) * length - depth
        point = jnp.arange(length + 2 * depth) + first
        inside = (point >= 0) & (point < length * lax.axis_size(axis))
        shape = [1, 1, 1]
        shape[dim] = length + 2 * depth
        mask = mask * inside.astype(jnp.float32).reshape(shape)
    return mask


def per_device(offsets, charge, counts, partners):
    slot_count = charge.shape[-1]
    cells_x, cells_y, cells_z = charge.shape[:3]
    in_use = (jnp.arange(slot_count) < counts[..., None]).astype(jnp.float32)
    weighted = charge * in_use
    packed = jnp.concatenate([offsets, weighted[None]], axis=0)
    grown_tiles = padded_2(packed, (("gx", 1), ("gy", 2), ("ga", 3)), 1)
    grown_offsets = grown_tiles[:3]
    grown_charge = grown_tiles[3]
    cell_units = cell_positions(grown_offsets, -1.0)
    grown = jnp.concatenate([cell_units, grown_charge[None]], axis=0)
    short_force = short_forces(counts, grown, partners)
    grid_x, grid_y, grid_z = (8 * cells_x, 8 * cells_y, 8 * cells_z)
    lengths = (grid_x, grid_y, grid_z)
    halo_depth = 10
    spread = spread_charge(offsets, weighted)
    widened = spread_halo(spread, (("ga", 2), ("gx", 0), ("gy", 1)), halo_depth)
    widened = widened * inside_mask(lengths, halo_depth)
    fine_potential = convolve(widened, fine_spread, fine_scale)
    known, coarse_depth = ((halo_depth - 1) // 2, 10)
    coarse_lengths = tuple(length // 2 for length in lengths)
    coarse_charge = widened
    for where_axis, fine_length in enumerate(lengths):
        coarse_charge = along_axis(
            coarse_charge,
            grid_map(
                fine_length + 2 * halo_depth,
                fine_length // 2 + 2 * known + 1,
                -halo_depth,
                -known,
            ),
            where_axis,
        )
    grown_coarse = coarse_halo(coarse_charge, (("ga", 2), ("gx", 0), ("gy", 1)), known, coarse_depth)
    grown_coarse = grown_coarse * inside_mask(coarse_lengths, coarse_depth)
    potential = convolve(grown_coarse, coarse_spread, coarse_scale)
    potential = potential * inside_mask(coarse_lengths, 2)
    for where_axis, fine_length in enumerate(lengths):
        potential = along_axis(
            potential,
            jnp.transpose(grid_map(fine_length + 4, fine_length // 2 + 4, -2, -2)),
            where_axis,
        )
    potential = (potential + fine_potential) * inside_mask(lengths, 2)
    long_force = grid_forces(offsets, weighted, potential)
    return (short_force, long_force)


def solution(mesh):
    return jax.shard_map(
        per_device,
        mesh=mesh,
        in_specs=(
            P(None, "gx", "gy", "ga", None),
            P("gx", "gy", "ga", None),
            P("gx", "gy", "ga"),
            P("gx", "gy", "ga", None),
        ),
        out_specs=(P(None, "gx", "gy", "ga", None), P(None, "gx", "gy", "ga", None)),
        check_vma=False,
    )
```

```python
import jax
import jax.numpy as jnp
from jax import lax
from jax.experimental import pallas as pl
from jax.experimental.pallas import tpu as pltpu
from jax.sharding import PartitionSpec as P

highest = lax.Precision.HIGHEST
bond_spring = 0.1
fine_scale = 4.0
coarse_scale = 2.0
fine_spread = 2.5
coarse_spread = 6.0


def padded_2(value, sides, width):
    for axis, dim in sides:
        size, length = (lax.axis_size(axis), value.shape[dim])
        up = [(i, (i + 1) % size) for i in range(size - 1)]
        down = [(j, i) for i, j in up]
        last = lax.slice_in_dim(value, length - width, length, axis=dim)
        initial = lax.slice_in_dim(value, 0, width, axis=dim)
        before = lax.ppermute(last, axis, up)
        after = lax.ppermute(initial, axis, down)
        value = jnp.concatenate([before, value, after], axis=dim)
    return value


def spline(shifted):
    magnitude = jnp.abs(shifted)
    margin = jnp.maximum(1.5 - magnitude, 0.0)
    return jnp.where(magnitude < 0.5, 0.75 - shifted * shifted, 0.5 * margin * margin)


def spline_slope(shifted):
    magnitude = jnp.abs(shifted)
    margin = jnp.maximum(1.5 - magnitude, 0.0)
    return jnp.where(magnitude < 0.5, -2.0 * shifted, jnp.where(shifted > 0.0, -margin, margin))


def split_product(left, right, dims):
    left_high, right_high = left.astype(jnp.bfloat16), right.astype(jnp.bfloat16)
    left_low = (left - left_high.astype(jnp.float32)).astype(jnp.bfloat16)
    right_low = (right - right_high.astype(jnp.float32)).astype(jnp.bfloat16)

    def product(one, other):
        return lax.dot_general(one, other, (dims, ((), ())), preferred_element_type=jnp.float32)

    return product(left_high, right_high) + (
        product(left_low, right_high) + product(left_high, right_low)
    )


def row_of_cells(ref, lead, k):
    return jnp.concatenate([ref[lead + (j, pl.ds(k, 1))] for j in range(ref.shape[-3])], axis=1)


def point_gaps(offset, count, shift):
    points = lax.broadcasted_iota(jnp.int32, (count, offset.shape[1]), 0).astype(jnp.float32)
    return (8.0 * offset + 1.0 + shift) - points


def cell_shift(cells_y, slots):
    lane = lax.broadcasted_iota(jnp.int32, (1, cells_y * slots), 1)
    return 8.0 * (lane // slots).astype(jnp.float32)


def spread_kernel(offsets_ref, weighted_ref, grid_ref):
    cells_x, cells_y, cells_z, slots = weighted_ref.shape
    width = grid_ref.shape[-1]
    grid_ref[...] = jnp.zeros_like(grid_ref)
    shift_y = cell_shift(cells_y, slots)

    def body(step, carry):
        i, k = step // cells_z, step % cells_z
        off_x, off_y, off_z = [row_of_cells(offsets_ref, (d, i), k) for d in range(3)]
        charge = row_of_cells(weighted_ref, (i,), k)
        weight_x = spline(point_gaps(off_x, 16, 0.0)) * charge
        weight_z = spline(point_gaps(off_z, 16, 0.0))
        weight_y = spline(point_gaps(off_y, width, shift_y))
        plane = jnp.concatenate([weight_x[a : a + 1] * weight_z for a in range(11)], axis=0)
        patch = split_product(plane, weight_y, ((1,), (1,)))
        for a in range(11):
            rows = pl.ds(pl.multiple_of(8 * k, 8), 16)
            grid_ref[8 * i + a, rows, :] += patch[16 * a : 16 * a + 16]
        return carry

    lax.fori_loop(0, cells_x * cells_z, body, 0)


def spread_charge(offsets, weighted):
    cells_x, cells_y, cells_z, _ = weighted.shape
    width = 8 * cells_y + 16
    grid = pl.pallas_call(
        spread_kernel,
        out_shape=jax.ShapeDtypeStruct((8 * cells_x + 3, 8 * cells_z + 8, width), jnp.float32),
        in_specs=[pl.BlockSpec(memory_space=pltpu.VMEM)] * 2,
        out_specs=pl.BlockSpec(memory_space=pltpu.VMEM),
        compiler_params=pltpu.CompilerParams(vmem_limit_bytes=24 * 2**20),
        cost_estimate=pl.CostEstimate(flops=10**8, bytes_accessed=4 * 10**6, transcendentals=0),
    )(offsets, weighted)
    return jnp.transpose(grid[:, : 8 * cells_z + 3, : 8 * cells_y + 3], (0, 2, 1))


def gather_kernel(offsets_ref, weighted_ref, grid_ref, out_ref):
    cells_x, cells_y, cells_z, slots = weighted_ref.shape
    width = grid_ref.shape[-1] // 3
    shift_y = cell_shift(cells_y, slots)
    lane = lax.broadcasted_iota(jnp.int32, (16, 3 * width), 1)
    middle = (lane >= width) & (lane < 2 * width)

    def body(step, carry):
        i, k = step // cells_z, step % cells_z
        off_x, off_y, off_z = [row_of_cells(offsets_ref, (d, i), k) for d in range(3)]
        gap_x, gap_z = point_gaps(off_x, 16, 0.0), point_gaps(off_z, 16, 0.0)
        gap_y = point_gaps(off_y, width, shift_y)
        weight_x, slope_x = spline(gap_x), spline_slope(gap_x)
        weight_z, slope_z = spline(gap_z), spline_slope(gap_z)
        both_y = jnp.concatenate([spline(gap_y), spline_slope(gap_y)], axis=1)
        y_high = both_y.astype(jnp.bfloat16)
        y_low = (both_y - y_high.astype(jnp.float32)).astype(jnp.bfloat16)
        parts = []
        for a in range(11):
            part = grid_ref[8 * i + a, pl.ds(pl.multiple_of(8 * k, 8), 16), :]
            low = part - part.astype(jnp.bfloat16).astype(jnp.float32)
            parts.append(jnp.where(middle, low, part).astype(jnp.bfloat16))
        found = jnp.dot(
            jnp.concatenate(parts, axis=0),
            jnp.concatenate([y_high, y_high, y_low], axis=0),
            preferred_element_type=jnp.float32,
        )
        lanes = cells_y * slots
        totals = [jnp.zeros((16, lanes), jnp.float32) for _ in range(3)]
        for a in range(11):
            level = found[16 * a : 16 * a + 16, :lanes]
            rising = found[16 * a : 16 * a + 16, lanes:]
            totals[0] += slope_x[a : a + 1] * level
            totals[1] += weight_x[a : a + 1] * rising
            totals[2] += weight_x[a : a + 1] * level
        charge = row_of_cells(weighted_ref, (i,), k)
        for d, along_z in enumerate((weight_z, weight_z, slope_z)):
            force = -charge * jnp.sum(totals[d] * along_z, axis=0, keepdims=True)
            for j in range(cells_y):
                out_ref[d, i, j, pl.ds(k, 1), :] = force[:, j * slots : (j + 1) * slots]
        return carry

    lax.fori_loop(0, cells_x * cells_z, body, 0)


def grid_forces(offsets, weighted, potential):
    cells_x, cells_y, cells_z, _ = weighted.shape
    width = 8 * cells_y + 16
    grid = jnp.transpose(potential[1:, 1:, 1:], (0, 2, 1))
    grid = jnp.pad(grid, ((0, 0), (0, 8 * cells_z + 8 - grid.shape[1]), (0, width - grid.shape[2])))
    grid = jnp.concatenate([grid] * 3, axis=2)
    return pl.pallas_call(
        gather_kernel,
        out_shape=jax.ShapeDtypeStruct(offsets.shape, jnp.float32),
        in_specs=[pl.BlockSpec(memory_space=pltpu.VMEM)] * 3,
        out_specs=pl.BlockSpec(memory_space=pltpu.VMEM),
        compiler_params=pltpu.CompilerParams(vmem_limit_bytes=24 * 2**20),
        cost_estimate=pl.CostEstimate(flops=10**8, bytes_accessed=4 * 10**6, transcendentals=0),
    )(offsets, weighted, grid)


def spread_halo(value, sides, depth):
    for axis, dim in sides:
        size, length = (lax.axis_size(axis), value.shape[dim] - 3)
        up = [(i, (i + 1) % size) for i in range(size - 1)]
        down = [(j, i) for i, j in up]
        last = lax.slice_in_dim(value, length - depth + 1, length + 3, axis=dim)
        initial = lax.slice_in_dim(value, 0, depth + 1, axis=dim)
        before = lax.ppermute(last, axis, up)
        after = lax.ppermute(initial, axis, down)

        def placed(part, low, high):
            widths = [(0, 0)] * part.ndim
            widths[dim] = (low, high)
            return jnp.pad(part, widths)

        value = (
            placed(value, depth - 1, depth - 2)
            + placed(before, 0, length + depth - 2)
            + placed(after, length + depth - 1, 0)
        )
    return value


def coarse_halo(value, sides, known, depth):
    for axis, dim in sides:
        size, length = (lax.axis_size(axis), value.shape[dim] - 2 * known - 1)
        up = [(i, (i + 1) % size) for i in range(size - 1)]
        down = [(j, i) for i, j in up]
        start = length - depth + known
        last = lax.slice_in_dim(value, start, start + depth - known, axis=dim)
        initial = lax.slice_in_dim(value, 2 * known + 1, depth + known, axis=dim)
        before = lax.ppermute(last, axis, up)
        after = lax.ppermute(initial, axis, down)
        value = jnp.concatenate([before, value, after], axis=dim)
    return value


def kernel_band(in_length, spread):
    row_index = jnp.arange(in_length)[:, None]
    column_index = jnp.arange(in_length - 16)[None, :]
    distance = row_index - column_index - 8
    gap = distance.astype(jnp.float32)
    return jnp.where(jnp.abs(distance) <= 8, jnp.exp(-gap * gap / (2.0 * spread * spread)), 0.0)


def along_axis(values, matrix, where_axis):
    contracted = jnp.tensordot(values, matrix, axes=([where_axis], [0]), precision=highest)
    return jnp.moveaxis(contracted, -1, where_axis)


def convolve(values, spread, strength):
    for where_axis in range(3):
        values = along_axis(values, kernel_band(values.shape[where_axis], spread), where_axis)
    return strength * values


def grid_map(fine_length, coarse_length, fine_start, coarse_start):
    fine_index = jnp.arange(fine_length)[:, None] + fine_start
    coarse_index = jnp.arange(coarse_length)[None, :] + coarse_start
    gap = fine_index - 2 * coarse_index
    return jnp.where(gap == 0, 1.0, jnp.where(jnp.abs(gap) == 1, 0.5, 0.0)).astype(jnp.float32)


def cell_positions(offsets, first_cell):
    coordinates = []
    for dimension in range(3):
        cell_count = offsets.shape[dimension + 1]
        cell_index = jnp.arange(cell_count).astype(jnp.float32) + first_cell
        broadcast_shape = [1, 1, 1, 1]
        broadcast_shape[dimension] = cell_count
        coordinates.append((cell_index.reshape(broadcast_shape) + offsets[dimension]))
    return jnp.stack(coordinates)


def short_kernel(counts_ref, grown_ref, partners_ref, out_ref, own_s, acc_s, near_s):
    _, cells_x, cells_y, cells_z, slots = out_ref.shape
    lane = lax.broadcasted_iota(jnp.int32, (1, slots), 1)

    def fill_body(column, carry):
        i, j = column // (cells_y + 2), column % (cells_y + 2)
        for k in range(cells_z + 2):
            for d in range(4):
                near_s[i, j, k, d] = jnp.broadcast_to(grown_ref[d, i, j, k : k + 1, :], (8, slots))
        return carry

    lax.fori_loop(0, (cells_x + 2) * (cells_y + 2), fill_body, 0)

    def cell_body(cell, carry):
        i = cell // (cells_y * cells_z)
        j = (cell // cells_z) % cells_y
        k = cell % cells_z
        count = counts_ref[cell]
        own_rows = [grown_ref[d, i + 1, j + 1, pl.ds(k + 1, 1), :] for d in range(3)]
        for d in range(3):
            own_s[d] = jnp.broadcast_to(own_rows[d], (slots, slots)).T

        def block_body(block, carry):
            rows = [pl.ds(pl.multiple_of(block * 16 + 8 * h, 8), 8) for h in range(2)]
            own = [[own_s[d, rows[h], :] for d in range(3)] for h in range(2)]
            total = [[jnp.zeros((8, slots), jnp.float32)] * 3 for _ in range(2)]
            for step_x in range(3):
                for step_y in range(3):
                    for step_z in range(3):
                        near = [
                            near_s[i + step_x, j + step_y, k + step_z, d] for d in range(4)
                        ]
                        for h in range(2):
                            gap = [own[h][d] - near[d] for d in range(3)]
                            distance_sq = gap[0] * gap[0] + gap[1] * gap[1] + gap[2] * gap[2]
                            reach = jnp.maximum(1.0 - distance_sq, 0.0)
                            inverse = pl.reciprocal(1.015625 - reach, approx=True)
                            strength = (reach * reach) * (reach * near[3]) * inverse
                            total[h] = [total[h][d] + strength * gap[d] for d in range(3)]
            for h in range(2):
                for d in range(3):
                    acc_s[d, rows[h], :] = total[h][d]
            return carry

        lax.fori_loop(0, (count + 15) // 16, block_body, 0)
        charge = grown_ref[3, i + 1, j + 1, pl.ds(k + 1, 1), :]
        partner = partners_ref[i, j, pl.ds(k, 1), :]
        bonded = (lane < count) & (partner < count)
        index = jnp.broadcast_to(partner, (8, slots))
        for d in range(3):
            pair = 0.125 * charge * jnp.sum(acc_s[d].T, axis=0, keepdims=True)
            source = jnp.broadcast_to(own_rows[d], (8, slots))
            other = jnp.take_along_axis(source, index, axis=1)[0:1]
            bond = jnp.where(bonded, (-8.0 * bond_spring) * (own_rows[d] - other), 0.0)
            out_ref[d, i, j, pl.ds(k, 1), :] = jnp.where(lane < count, pair, 0.0) + bond
        return carry

    lax.fori_loop(0, cells_x * cells_y * cells_z, cell_body, 0)


def short_forces(counts, grown, partners):
    cells, slots = counts.shape, partners.shape[-1]
    return pl.pallas_call(
        short_kernel,
        out_shape=jax.ShapeDtypeStruct((3,) + cells + (slots,), jnp.float32),
        in_specs=[pl.BlockSpec(memory_space=pltpu.SMEM)]
        + [pl.BlockSpec(memory_space=pltpu.VMEM)] * 2,
        out_specs=pl.BlockSpec(memory_space=pltpu.VMEM),
        scratch_shapes=[pltpu.VMEM((3, slots, slots), jnp.float32)] * 2
        + [pltpu.VMEM(grown.shape[1:4] + (4, 8, slots), jnp.float32)],
        compiler_params=pltpu.CompilerParams(vmem_limit_bytes=24 * 2**20),
        cost_estimate=pl.CostEstimate(flops=10**9, bytes_accessed=10**7, transcendentals=10**7),
    )(counts.reshape(-1), grown, partners)


def inside_mask(lengths, depth):
    mask = jnp.float32(1.0)
    for dim, axis in enumerate(("gx", "gy", "ga")):
        length = lengths[dim]
        first = lax.axis_index(axis) * length - depth
        point = jnp.arange(length + 2 * depth) + first
        inside = (point >= 0) & (point < length * lax.axis_size(axis))
        shape = [1, 1, 1]
        shape[dim] = length + 2 * depth
        mask = mask * inside.astype(jnp.float32).reshape(shape)
    return mask


def per_device(offsets, charge, counts, partners):
    slot_count = charge.shape[-1]
    cells_x, cells_y, cells_z = charge.shape[:3]
    in_use = (jnp.arange(slot_count) < counts[..., None]).astype(jnp.float32)
    weighted = charge * in_use
    packed = jnp.concatenate([offsets, weighted[None]], axis=0)
    grown_tiles = padded_2(packed, (("gx", 1), ("gy", 2), ("ga", 3)), 1)
    grown_offsets = grown_tiles[:3]
    grown_charge = grown_tiles[3]
    cell_units = cell_positions(grown_offsets, -1.0)
    grown = jnp.concatenate([cell_units, grown_charge[None]], axis=0)
    short_force = short_forces(counts, grown, partners)
    grid_x, grid_y, grid_z = (8 * cells_x, 8 * cells_y, 8 * cells_z)
    lengths = (grid_x, grid_y, grid_z)
    halo_depth = 10
    spread = spread_charge(offsets, weighted)
    widened = spread_halo(spread, (("ga", 2), ("gx", 0), ("gy", 1)), halo_depth)
    widened = widened * inside_mask(lengths, halo_depth)
    fine_potential = convolve(widened, fine_spread, fine_scale)
    known, coarse_depth = ((halo_depth - 1) // 2, 10)
    coarse_lengths = tuple(length // 2 for length in lengths)
    coarse_charge = widened
    for where_axis, fine_length in enumerate(lengths):
        coarse_charge = along_axis(
            coarse_charge,
            grid_map(
                fine_length + 2 * halo_depth,
                fine_length // 2 + 2 * known + 1,
                -halo_depth,
                -known,
            ),
            where_axis,
        )
    grown_coarse = coarse_halo(coarse_charge, (("ga", 2), ("gx", 0), ("gy", 1)), known, coarse_depth)
    grown_coarse = grown_coarse * inside_mask(coarse_lengths, coarse_depth)
    potential = convolve(grown_coarse, coarse_spread, coarse_scale)
    potential = potential * inside_mask(coarse_lengths, 2)
    for where_axis, fine_length in enumerate(lengths):
        potential = along_axis(
            potential,
            jnp.transpose(grid_map(fine_length + 4, fine_length // 2 + 4, -2, -2)),
            where_axis,
        )
    potential = (potential + fine_potential) * inside_mask(lengths, 2)
    long_force = grid_forces(offsets, weighted, potential)
    return (short_force, long_force)


def solution(mesh):
    return jax.shard_map(
        per_device,
        mesh=mesh,
        in_specs=(
            P(None, "gx", "gy", "ga", None),
            P("gx", "gy", "ga", None),
            P("gx", "gy", "ga"),
            P("gx", "gy", "ga", None),
        ),
        out_specs=(P(None, "gx", "gy", "ga", None), P(None, "gx", "gy", "ga", None)),
        check_vma=False,
    )
```
